32 devices in a mesh: inline: 2 (over y), window: 4 (over z), replica: 4 (over x, core).
Axes of the slice: x: 2, y: 2, z: 4, core: 2. Of those that a mesh axis runs over, the one named last changes fastest.
Arguments:
- tokens: bfloat16 [64, 128, 8, 512], P(('replica', 'inline', 'window')), parts along dimension 0, may hold values from -6 to 6
- probe_match_payload_matrix: bfloat16 [512, 1536], replicated, may hold values from -1.5 to 1.5
- w_out: bfloat16 [512, 512], replicated, may hold values from -0.25 to 0.25
Outputs:
- update: bfloat16 [64, 128, 8, 512], P(('replica', 'inline', 'window')), parts along dimension 0
The draws below stay inside these ranges and needn't reach their ends.
There are 4 independent parts, one for each index of `replica`. The reference program is written for one: setup_inputs(seed, part) draws one part's arguments, and reference() takes and returns one part's arrays. A program takes and returns all parts, laid end to end along the dimension named above; an argument that names none is the same for every part. Nothing has to cross between parts.
All inputs are finite; a program needn't handle non-finite values.
Results may differ from the reference program's by a relative error of at most 0.012.
The reference program's roundings to bfloat16 on the way count: a program that leaves them out, or rounds other values in their place, can miss the bound.
Values may be sent and summed in bfloat16 or wider, within the bound.
A program may use at most 64 MiB of HBM per device.

```python
import jax
import jax.numpy as jnp
from jax import lax

EMBED_SPAN = 512
FOCUS_GROUPS = 16
WIN = 8
XL = 128
DEP = 8
INL = 16
TILE_TOTAL = 32


def draw_probe_match_payload_matrix(key, part):
    first, second, third = jax.random.split(jax.random.fold_in(key, 7), 3)
    width = EMBED_SPAN
    payload_vectors = jax.random.normal(third, (width, width), jnp.float32) / jnp.sqrt(1.0 * width)
    question_arrays = jax.random.normal(first, (width, width), jnp.float32) * (1.5 / jnp.sqrt(1.0 * width))
    lookup_arrays = jax.random.normal(second, (width, width), jnp.float32) * (1.5 / jnp.sqrt(1.0 * width))
    joined = jnp.concatenate([question_arrays, lookup_arrays, payload_vectors], axis=1)
    return jnp.clip(joined, -1.5, 1.5).astype(jnp.bfloat16)


def shard_levels(rng, dims, pieces, least, top_value):
    loudness = 1.0
    for axis_at, shards_of in pieces:
        draws = jax.random.uniform(jax.random.fold_in(jax.random.fold_in(rng, 6), axis_at), (shards_of,), jnp.float32, least / len(pieces), top_value / len(pieces))
        loudness = loudness * jnp.repeat(jnp.exp(draws), dims[axis_at] // shards_of).reshape((-1,) + (1,) * (len(dims) - 1 - axis_at))
    return loudness


def centred(stream_key, dims, scale, most, pieces=(), kind=jnp.bfloat16):
    values = scale * jax.random.normal(stream_key, dims, jnp.float32)
    if pieces:
        values = values * shard_levels(stream_key, dims, pieces, -0.22, 0.18)
    return jnp.clip(values, -most, most).astype(kind)


def setup_inputs(seed: int = 0, part: int = 0) -> dict:
    seeds = jax.random.split(jax.random.key(seed), 4)
    own_keys = jax.random.split(jax.random.fold_in(seeds[3], part), 4)
    return {
        "tokens": centred(own_keys[0], (INL, XL, DEP, EMBED_SPAN), 1.0, 6.0, ((0, 8),)),
        "probe_match_payload_matrix": draw_probe_match_payload_matrix(jax.random.fold_in(seeds[3], 71), part),
        "w_out": centred(seeds[2], (EMBED_SPAN, EMBED_SPAN), EMBED_SPAN ** -0.5, 0.25),
    }


EPSILON = 1e-05

def standardize_features(payload_vectors):
    center = payload_vectors - lax.optimization_barrier(jnp.mean(payload_vectors, axis=-1, keepdims=True))
    spread = lax.optimization_barrier(jnp.mean(center * center, axis=-1, keepdims=True))
    return center * lax.rsqrt(spread + EPSILON)

def round_trip(payload_vectors):
    return lax.optimization_barrier(payload_vectors.astype(jnp.bfloat16)).astype(jnp.float32)

def to_windows(block):
    first, second, third, width = block.shape
    shaped = block.reshape(first // WIN, WIN, second // WIN, WIN, third // WIN, WIN, width)
    return shaped.transpose(0, 2, 4, 1, 3, 5, 6).reshape(-1, WIN * WIN * WIN, width)

def from_windows(cube_rows, first, second, third):
    width = cube_rows.shape[-1]
    shaped = cube_rows.reshape(first // WIN, second // WIN, third // WIN, WIN, WIN, WIN, width)
    return shaped.transpose(0, 3, 1, 4, 2, 5, 6).reshape(first, second, third, width)

def tile_mixing(tile_items, probe_match_payload_matrix, digest_match_list, digest_payload_list, broad_contribution):
    count = tile_items.shape[0]
    reduced_dimension = EMBED_SPAN // FOCUS_GROUPS
    softmax_sharpness = reduced_dimension ** (-0.5)
    projected = jnp.dot(tile_items, probe_match_payload_matrix, preferred_element_type=jnp.float32).astype(jnp.bfloat16)
    question_arrays = projected[:, :EMBED_SPAN].reshape(count, FOCUS_GROUPS, reduced_dimension).astype(jnp.float32)
    lookup_arrays = projected[:, EMBED_SPAN:2 * EMBED_SPAN].reshape(count, FOCUS_GROUPS, reduced_dimension).astype(jnp.float32)
    payload_vectors = projected[:, 2 * EMBED_SPAN:].reshape(count, FOCUS_GROUPS, reduced_dimension).astype(jnp.float32)
    lookup_condensed = digest_match_list.reshape(FOCUS_GROUPS, reduced_dimension).astype(jnp.float32)
    payload_digest = digest_payload_list.reshape(FOCUS_GROUPS, reduced_dimension).astype(jnp.float32)
    per_group = FOCUS_GROUPS // 4
    results = []
    for head_group in range(4):
        bottom_bound = head_group * per_group
        ceiling_bound = bottom_bound + per_group
        similarity_raw_scores = jnp.einsum('xjr,ijr->jxi', question_arrays[:, bottom_bound:ceiling_bound], lookup_arrays[:, bottom_bound:ceiling_bound]) * softmax_sharpness
        courier_marks = jnp.einsum('yoc,oc->oy', question_arrays[:, bottom_bound:ceiling_bound], lookup_condensed[bottom_bound:ceiling_bound]) * softmax_sharpness
        top = jnp.maximum(lax.optimization_barrier(jnp.max(similarity_raw_scores, axis=-1)), courier_marks)
        weights = jnp.exp(similarity_raw_scores - top[..., None])
        car_weights = jnp.exp(courier_marks - top)
        total = lax.optimization_barrier(jnp.sum(weights, axis=-1)) + car_weights
        summed = jnp.einsum('hqk,khd->qhd', round_trip(weights), payload_vectors[:, bottom_bound:ceiling_bound])
        summed = summed + round_trip(car_weights).T[:, :, None] * payload_digest[bottom_bound:ceiling_bound][None, :, :]
        results.append(summed / total.T[:, :, None])
    local = jnp.concatenate(results, axis=1).reshape(count, EMBED_SPAN)
    return (local + broad_contribution[None, :]).astype(jnp.bfloat16)

def reference(tokens, probe_match_payload_matrix, w_out):
    reduced_dimension = EMBED_SPAN // FOCUS_GROUPS
    softmax_sharpness = reduced_dimension ** (-0.5)
    normed = standardize_features(tokens.astype(jnp.float32)).astype(jnp.bfloat16)
    tile_entries = to_windows(normed)
    averaged_tiles = lax.optimization_barrier(jnp.mean(tile_entries.astype(jnp.float32), axis=1))
    digest_items = standardize_features(averaged_tiles).astype(jnp.bfloat16)
    digest_mapping = jnp.dot(digest_items, probe_match_payload_matrix, preferred_element_type=jnp.float32).astype(jnp.bfloat16)
    condensed_question_series = digest_mapping[:, :EMBED_SPAN].reshape(TILE_TOTAL, FOCUS_GROUPS, reduced_dimension).astype(jnp.float32)
    digest_match_list = digest_mapping[:, EMBED_SPAN:2 * EMBED_SPAN]
    digest_payload_list = digest_mapping[:, 2 * EMBED_SPAN:]
    lookup_divided = digest_match_list.reshape(TILE_TOTAL, FOCUS_GROUPS, reduced_dimension).astype(jnp.float32)
    payload_split = digest_payload_list.reshape(TILE_TOTAL, FOCUS_GROUPS, reduced_dimension).astype(jnp.float32)
    similarity_raw_scores = jnp.einsum('xjr,ijr->jxi', condensed_question_series, lookup_divided) * softmax_sharpness
    top = lax.optimization_barrier(jnp.max(similarity_raw_scores, axis=-1, keepdims=True))
    weights = jnp.exp(similarity_raw_scores - top)
    total = lax.optimization_barrier(jnp.sum(weights, axis=-1))
    summed = jnp.einsum('hqk,khd->qhd', round_trip(weights), payload_split)
    broad_context = (summed / total.T[:, :, None]).reshape(TILE_TOTAL, EMBED_SPAN)

    def single_tile(window_item):
        nested_step = tile_mixing(window_item[0], probe_match_payload_matrix, window_item[1], window_item[2], window_item[3])
        return jnp.dot(nested_step, w_out, preferred_element_type=jnp.float32).astype(jnp.bfloat16)
    increments = lax.map(single_tile, (tile_entries, digest_match_list, digest_payload_list, broad_context))
    return from_windows(increments, INL, XL, DEP)
```

```python
import functools

import jax
import jax.numpy as jnp
from jax import lax
from jax.experimental import pallas as pl
from jax.experimental.pallas import tpu as pltpu
from jax.sharding import PartitionSpec as P

EMBED_SPAN = 512
FOCUS_GROUPS = 16
HEAD = EMBED_SPAN // FOCUS_GROUPS
WIN = 8
EPSILON = 1e-05
MESH = pl.DeviceIdType.MESH
F32 = jnp.float32
BF16 = jnp.bfloat16


def standardize(x):
    center = x - jnp.mean(x, axis=-1, keepdims=True)
    spread = jnp.mean(center * center, axis=-1, keepdims=True)
    return center * lax.rsqrt(spread + EPSILON)


def window_peers(me, n):
    if n % 2:
        return [lax.rem(me + o, n) for o in range(1, n)]
    same = [lax.rem(me + o, n) for o in range(2, n, 2)]
    odd = [lax.rem(n + c - me, n) for c in range(n - 1, 0, -2)]
    return same + odd


def kernel(
    n_in, n_win, rows, strips,
    tok_ref, w_ref, wo_ref, out_ref,
    normed, xin, ybuf, psum, cars, wq_t, wv_t, k_buf, q_t, v_t, in_t, glob_buf, kcar_buf, vcar_buf,
    fsend, frecv, bsend, brecv, psend, precv, csend, crecv, lsem, blsem,
):
    ii = lax.axis_index("inline")
    me = lax.axis_index("window")
    span = strips // n_win
    npos = WIN // rows
    n_ci = n_win // npos
    own = span * n_ci
    group_cars = n_ci * strips
    width = EMBED_SPAN
    tokens = WIN * WIN * WIN
    my_ci = me // npos
    my_pos = lax.rem(me, npos)
    peers = window_peers(me, n_win)
    in_peers = [lax.rem(ii + o, n_in) for o in range(1, n_in)]

    barrier = pltpu.get_barrier_semaphore()
    for d in peers:
        pl.semaphore_signal(barrier, inc=1, device_id={"window": d}, device_id_type=MESH)
    for d in in_peers:
        pl.semaphore_signal(barrier, inc=1, device_id={"inline": d}, device_id_type=MESH)

    def norm_strip(cx, carry):
        x = standardize(tok_ref[:, cx].astype(F32)).astype(BF16)
        normed[cx] = x
        part = jnp.sum(x.astype(F32), axis=(0, 1))
        psum[me, pl.ds(cx, 1), :] = part[None, :]
        return carry

    lax.fori_loop(0, strips, norm_strip, 0)
    pl.semaphore_wait(barrier, len(peers) + len(in_peers))

    def p_copy(k, d, src):
        return pltpu.make_async_remote_copy(
            src_ref=psum.at[src], dst_ref=psum.at[src], send_sem=psend.at[k], recv_sem=precv.at[src],
            device_id={"window": d}, device_id_type=MESH,
        )

    def f_copy(k, j, d, src):
        return pltpu.make_async_remote_copy(
            src_ref=normed.at[d * span + j], dst_ref=xin.at[(src // npos) * span + j, lax.rem(src, npos)],
            send_sem=fsend.at[k, j], recv_sem=frecv.at[src, j],
            device_id={"window": d}, device_id_type=MESH,
        )

    def l_copy(j):
        return pltpu.make_async_copy(
            normed.at[me * span + j], xin.at[my_ci * span + j, my_pos], lsem.at[j]
        )

    for k, d in enumerate(peers):
        p_copy(k, d, me).start()
    for j in range(span):
        for k, d in enumerate(peers):
            f_copy(k, j, d, me).start()
        l_copy(j).start()

    wq_t[...] = w_ref[:, :width].T
    wv_t[...] = w_ref[:, 2 * width :].T

    for d in peers:
        p_copy(0, d, d).wait_recv()
    for ci in range(n_ci):
        total = psum[ci * npos]
        for p in range(1, npos):
            total = total + psum[ci * npos + p]
        cars[ii, pl.ds(ci * strips, strips), :] = standardize(total * (1.0 / tokens)).astype(BF16)

    def c_copy(k, d, src):
        return pltpu.make_async_remote_copy(
            src_ref=cars.at[src], dst_ref=cars.at[src], send_sem=csend.at[k], recv_sem=crecv.at[src],
            device_id={"inline": d}, device_id_type=MESH,
        )

    for k, d in enumerate(in_peers):
        c_copy(k, d, ii).start()

    scale = HEAD ** (-0.5)
    mine = jnp.dot(cars[ii], w_ref[...], preferred_element_type=F32).astype(BF16)
    kcar_buf[...] = mine[:, width : 2 * width].astype(F32)
    vcar_buf[...] = mine[:, 2 * width :].astype(F32)
    for d in in_peers:
        c_copy(0, d, d).wait_recv()
    every = cars[...].reshape(n_in * group_cars, width)
    kv = jnp.dot(every, w_ref[:, width:], preferred_element_type=F32).astype(BF16)
    col_head = lax.broadcasted_iota(jnp.int32, (group_cars, width), 1) // HEAD
    q_car = mine[:, :width].astype(F32)
    glob = jnp.zeros((group_cars, width), F32)
    for h in range(FOCUS_GROUPS):
        q_h = jnp.where(col_head == h, q_car, 0.0).astype(BF16)
        s = lax.dot_general(q_h, kv[:, :width], (((1,), (1,)), ((), ())), preferred_element_type=F32) * scale
        e = jnp.exp(s - jnp.max(s, axis=-1, keepdims=True))
        t = jnp.sum(e, axis=-1, keepdims=True)
        o = jnp.dot(e.astype(BF16), kv[:, width:], preferred_element_type=F32) / t
        glob = jnp.where(col_head == h, o, glob)
    glob_buf[...] = glob

    def b_copy(slot, p, dst, owner, j):
        return pltpu.make_async_remote_copy(
            src_ref=ybuf.at[slot, p], dst_ref=out_ref.at[:, owner * span + j],
            send_sem=bsend.at[slot, p], recv_sem=brecv.at[owner, j],
            device_id={"window": dst}, device_id_type=MESH,
        )

    def bl_copy(slot, j):
        return pltpu.make_async_copy(ybuf.at[slot, my_pos], out_ref.at[:, me * span + j], blsem.at[j])

    def cube(slot, carry):
        ci = slot // span
        j = lax.rem(slot, span)
        for p in range(npos):
            src = ci * npos + p

            @pl.when(src != me)
            def _():
                f_copy(0, j, me, src).wait_recv()

            @pl.when(src == me)
            def _():
                l_copy(j).wait()

        x = xin[slot].reshape(tokens, width)
        row = ci * strips + me * span + j
        pick = lax.broadcasted_iota(jnp.int32, (group_cars, width), 0) == row

        def chosen(ref):
            return jnp.sum(jnp.where(pick, ref[...], 0.0), axis=0, keepdims=True)

        def column(r):
            return jnp.broadcast_to(r, (128, width)).T[:, :1]

        k_buf[:tokens, :] = jnp.dot(x, w_ref[:, width : 2 * width], preferred_element_type=F32).astype(BF16)
        k_buf[tokens:, :] = jnp.broadcast_to(chosen(kcar_buf), (16, width)).astype(BF16)
        nt = (((1,), (1,)), ((), ()))
        q_t[...] = lax.dot_general(wq_t[...], x, nt, preferred_element_type=F32).astype(BF16)
        v_t[...] = lax.dot_general(wv_t[...], x, nt, preferred_element_type=F32).astype(BF16)
        glob_col = column(chosen(glob_buf))
        vcar_col = column(chosen(vcar_buf))
        for hb in range(width // 128):
            kb = k_buf[:, hb * 128 : (hb + 1) * 128]
            for h4 in range(128 // HEAD):
                lo = hb * 128 + h4 * HEAD
                parts = [q_t[lo : lo + HEAD, :]]
                if h4:
                    parts.insert(0, jnp.zeros((h4 * HEAD, tokens), BF16))
                if h4 < 128 // HEAD - 1:
                    parts.append(jnp.zeros((128 - (h4 + 1) * HEAD, tokens), BF16))
                s = jnp.dot(kb, jnp.concatenate(parts, axis=0), preferred_element_type=F32)
                s_car = s[tokens : tokens + 1]
                s = s[:tokens]
                top = jnp.maximum(jnp.max(s, axis=0, keepdims=True), s_car)
                e = jnp.exp((s - top) * scale)
                e_car = jnp.exp((s_car - top) * scale)
                total = jnp.sum(e, axis=0, keepdims=True) + e_car
                o = jnp.dot(v_t[lo : lo + HEAD, :], e.astype(BF16), preferred_element_type=F32)
                o = o + vcar_col[lo : lo + HEAD] * e_car.astype(BF16).astype(F32)
                in_t[lo : lo + HEAD, :] = (o / total + glob_col[lo : lo + HEAD]).astype(BF16)
        inner = in_t[...].T
        upd = jnp.dot(inner, wo_ref[...], preferred_element_type=F32).astype(BF16)
        ybuf[slot] = upd.reshape(npos, rows, WIN * WIN, width)
        for p in range(npos):
            dst = ci * npos + p

            @pl.when(dst != me)
            def _():
                b_copy(slot, p, dst, me, j).start()

            @pl.when(dst == me)
            def _():
                bl_copy(slot, j).start()

        return carry

    lax.fori_loop(0, own, cube, 0)

    for k, d in enumerate(peers):
        p_copy(k, d, me).wait_send()
    for k, d in enumerate(in_peers):
        c_copy(k, d, ii).wait_send()
    for j in range(span):
        for k, d in enumerate(peers):
            f_copy(k, j, d, me).wait_send()
    for j in range(span):
        for d in peers:
            b_copy(0, 0, me, d, j).wait_recv()
        bl_copy(my_ci * span + j, j).wait()
    for slot in range(own):
        for p in range(npos):
            dst = (slot // span) * npos + p

            @pl.when(dst != me)
            def _():
                b_copy(slot, p, dst, me, slot % span).wait_send()


def body(n_in, n_win, tokens, w, w_out):
    rows, xl, dep, width = tokens.shape
    strips = xl // WIN
    npos = WIN // rows
    span = strips // n_win
    own = span * (n_win // npos)
    group_cars = (n_win // npos) * strips
    cube = WIN * WIN * WIN
    block = (rows, WIN * WIN, width)
    vmem = pl.BlockSpec(memory_space=pltpu.VMEM)
    dma = pltpu.SemaphoreType.DMA
    shaped = tokens.reshape(rows, strips, WIN * dep, width)
    out = pl.pallas_call(
        functools.partial(kernel, n_in, n_win, rows, strips),
        out_shape=jax.ShapeDtypeStruct(shaped.shape, BF16),
        in_specs=[vmem, vmem, vmem],
        out_specs=pl.BlockSpec(memory_space=pl.ANY),
        scratch_shapes=[
            pltpu.VMEM((strips,) + block, BF16),
            pltpu.VMEM((own, npos) + block, BF16),
            pltpu.VMEM((own, npos) + block, BF16),
            pltpu.VMEM((n_win, strips, width), F32),
            pltpu.VMEM((n_in, group_cars, width), BF16),
            pltpu.VMEM((width, width), BF16),
            pltpu.VMEM((width, width), BF16),
            pltpu.VMEM((cube + 16, width), BF16),
            pltpu.VMEM((width, cube), BF16),
            pltpu.VMEM((width, cube), BF16),
            pltpu.VMEM((width, cube), BF16),
            pltpu.VMEM((group_cars, width), F32),
            pltpu.VMEM((group_cars, width), F32),
            pltpu.VMEM((group_cars, width), F32),
            dma((n_win, span)),
            dma((n_win, span)),
            dma((own, npos)),
            dma((n_win, span)),
            dma((n_win,)),
            dma((n_win,)),
            dma((n_in,)),
            dma((n_in,)),
            dma((span,)),
            dma((span,)),
        ],
        compiler_params=pltpu.CompilerParams(
            collective_id=0, has_side_effects=True, vmem_limit_bytes=48 * 1024 * 1024
        ),
        cost_estimate=pl.CostEstimate(
            flops=2 * own * cube * width * (4 * width + 2 * cube),
            bytes_accessed=4 * own * cube * width,
            transcendentals=own * FOCUS_GROUPS * cube * cube,
        ),
    )(shaped, w, w_out)
    return out.reshape(tokens.shape)


def solution(mesh):
    return jax.shard_map(
        functools.partial(body, mesh.shape["inline"], mesh.shape["window"]),
        mesh=mesh,
        in_specs=(P(("replica", "inline", "window"), None, None, None), P(), P()),
        out_specs=P(("replica", "inline", "window"), None, None, None),
        check_vma=False,
    )
```

```python
import functools

import jax
import jax.numpy as jnp
from jax import lax
from jax.experimental import pallas as pl
from jax.experimental.pallas import tpu as pltpu
from jax.sharding import PartitionSpec as P

EMBED_SPAN = 512
FOCUS_GROUPS = 16
HEAD = EMBED_SPAN // FOCUS_GROUPS
WIN = 8
EPSILON = 1e-05
MESH = pl.DeviceIdType.MESH
F32 = jnp.float32
BF16 = jnp.bfloat16


def standardize(x):
    center = x - jnp.mean(x, axis=-1, keepdims=True)
    spread = jnp.mean(center * center, axis=-1, keepdims=True)
    return center * lax.rsqrt(spread + EPSILON)


def window_peers(me, n):
    if n % 2:
        return [lax.rem(me + o, n) for o in range(1, n)]
    same = [lax.rem(me + o, n) for o in range(2, n, 2)]
    odd = [lax.rem(n + c - me, n) for c in range(n - 1, 0, -2)]
    return same + odd


def kernel(
    n_in, n_win, rows, strips,
    tok_ref, w_hbm, wo_hbm, out_ref,
    tok_buf, w_ref, wo_ref,
    normed, xin, ybuf, psum, cars, wq_t, wv_t, k_buf, q_t, v_t, in_t, glob_buf, kcar_buf, vcar_buf,
    fsend, frecv, bsend, brecv, psend, precv, csend, crecv, lsem, blsem, tsem, wsem,
):
    ii = lax.axis_index("inline")
    me = lax.axis_index("window")
    span = strips // n_win
    npos = WIN // rows
    n_ci = n_win // npos
    own = span * n_ci
    group_cars = n_ci * strips
    width = EMBED_SPAN
    tokens = WIN * WIN * WIN
    my_ci = me // npos
    my_pos = lax.rem(me, npos)
    peers = window_peers(me, n_win)
    in_peers = [lax.rem(ii + o, n_in) for o in range(1, n_in)]

    barrier = pltpu.get_barrier_semaphore()
    for d in peers:
        pl.semaphore_signal(barrier, inc=1, device_id={"window": d}, device_id_type=MESH)
    for d in in_peers:
        pl.semaphore_signal(barrier, inc=1, device_id={"inline": d}, device_id_type=MESH)

    order = [(j, k, d) for j in range(span) for k, d in enumerate(peers + [me])]

    def t_copy(n):
        j, _, d = order[n]
        return pltpu.make_async_copy(tok_ref.at[:, d * span + j], tok_buf.at[n], tsem.at[n])

    for n in range(len(order)):
        t_copy(n).start()
    w_copy = pltpu.make_async_copy(w_hbm, w_ref, wsem.at[0])
    wo_copy = pltpu.make_async_copy(wo_hbm, wo_ref, wsem.at[1])
    w_copy.start()
    wo_copy.start()

    def p_copy(k, d, src):
        return pltpu.make_async_remote_copy(
            src_ref=psum.at[src], dst_ref=psum.at[src], send_sem=psend.at[k], recv_sem=precv.at[src],
            device_id={"window": d}, device_id_type=MESH,
        )

    def f_copy(k, j, d, src):
        return pltpu.make_async_remote_copy(
            src_ref=normed.at[d * span + j], dst_ref=xin.at[(src // npos) * span + j, lax.rem(src, npos)],
            send_sem=fsend.at[k, j], recv_sem=frecv.at[src, j],
            device_id={"window": d}, device_id_type=MESH,
        )

    def l_copy(j):
        return pltpu.make_async_copy(
            normed.at[me * span + j], xin.at[my_ci * span + j, my_pos], lsem.at[j]
        )

    for n, (j, k, d) in enumerate(order):
        t_copy(n).wait()
        x = standardize(tok_buf[n].astype(F32)).astype(BF16)
        normed[d * span + j] = x
        psum[me, pl.ds(d * span + j, 1), :] = jnp.sum(x.astype(F32), axis=(0, 1))[None, :]
        if n == 0:
            pl.semaphore_wait(barrier, len(peers) + len(in_peers))
        if j == 0:
            if k == len(peers):
                l_copy(j).start()
            else:
                f_copy(k, j, d, me).start()
    for k, d in enumerate(peers):
        p_copy(k, d, me).start()
    for j, k, d in order:
        if j:
            if k == len(peers):
                l_copy(j).start()
            else:
                f_copy(k, j, d, me).start()
    w_copy.wait()
    wo_copy.wait()

    wq_t[...] = w_ref[:, :width].T
    wv_t[...] = w_ref[:, 2 * width :].T

    for d in peers:
        p_copy(0, d, d).wait_recv()
    for ci in range(n_ci):
        total = psum[ci * npos]
        for p in range(1, npos):
            total = total + psum[ci * npos + p]
        cars[ii, pl.ds(ci * strips, strips), :] = standardize(total * (1.0 / tokens)).astype(BF16)

    def c_copy(k, d, src):
        return pltpu.make_async_remote_copy(
            src_ref=cars.at[src], dst_ref=cars.at[src], send_sem=csend.at[k], recv_sem=crecv.at[src],
            device_id={"inline": d}, device_id_type=MESH,
        )

    for k, d in enumerate(in_peers):
        c_copy(k, d, ii).start()

    scale = HEAD ** (-0.5)
    mine = jnp.dot(cars[ii], w_ref[...], preferred_element_type=F32).astype(BF16)
    kcar_buf[...] = mine[:, width : 2 * width].astype(F32)
    vcar_buf[...] = mine[:, 2 * width :].astype(F32)
    for d in in_peers:
        c_copy(0, d, d).wait_recv()
    every = cars[...].reshape(n_in * group_cars, width)
    kv = jnp.dot(every, w_ref[:, width:], preferred_element_type=F32).astype(BF16)
    col_head = lax.broadcasted_iota(jnp.int32, (group_cars, width), 1) // HEAD
    q_car = mine[:, :width].astype(F32)
    glob = jnp.zeros((group_cars, width), F32)
    for h in range(FOCUS_GROUPS):
        q_h = jnp.where(col_head == h, q_car, 0.0).astype(BF16)
        s = lax.dot_general(q_h, kv[:, :width], (((1,), (1,)), ((), ())), preferred_element_type=F32) * scale
        e = jnp.exp(s - jnp.max(s, axis=-1, keepdims=True))
        t = jnp.sum(e, axis=-1, keepdims=True)
        o = jnp.dot(e.astype(BF16), kv[:, width:], preferred_element_type=F32) / t
        glob = jnp.where(col_head == h, o, glob)
    glob_buf[...] = glob

    def b_copy(slot, p, dst, owner, j):
        return pltpu.make_async_remote_copy(
            src_ref=ybuf.at[slot, p], dst_ref=out_ref.at[:, owner * span + j],
            send_sem=bsend.at[slot, p], recv_sem=brecv.at[owner, j],
            device_id={"window": dst}, device_id_type=MESH,
        )

    def bl_copy(slot, j):
        return pltpu.make_async_copy(ybuf.at[slot, my_pos], out_ref.at[:, me * span + j], blsem.at[j])

    def cube(slot, carry):
        ci = slot // span
        j = lax.rem(slot, span)
        for p in range(npos):
            src = ci * npos + p

            @pl.when(src != me)
            def _():
                f_copy(0, j, me, src).wait_recv()

            @pl.when(src == me)
            def _():
                l_copy(j).wait()

        x = xin[slot].reshape(tokens, width)
        row = ci * strips + me * span + j
        pick = lax.broadcasted_iota(jnp.int32, (group_cars, width), 0) == row

        def chosen(ref):
            return jnp.sum(jnp.where(pick, ref[...], 0.0), axis=0, keepdims=True)

        def column(r):
            return jnp.broadcast_to(r, (128, width)).T[:, :1]

        k_buf[:tokens, :] = jnp.dot(x, w_ref[:, width : 2 * width], preferred_element_type=F32).astype(BF16)
        k_buf[tokens:, :] = jnp.broadcast_to(chosen(kcar_buf), (16, width)).astype(BF16)
        nt = (((1,), (1,)), ((), ()))
        q_t[...] = lax.dot_general(wq_t[...], x, nt, preferred_element_type=F32).astype(BF16)
        v_t[...] = lax.dot_general(wv_t[...], x, nt, preferred_element_type=F32).astype(BF16)
        glob_col = column(chosen(glob_buf))
        vcar_col = column(chosen(vcar_buf))
        for hb in range(width // 128):
            kb = k_buf[:, hb * 128 : (hb + 1) * 128]
            for h4 in range(128 // HEAD):
                lo = hb * 128 + h4 * HEAD
                parts = [q_t[lo : lo + HEAD, :]]
                if h4:
                    parts.insert(0, jnp.zeros((h4 * HEAD, tokens), BF16))
                if h4 < 128 // HEAD - 1:
                    parts.append(jnp.zeros((128 - (h4 + 1) * HEAD, tokens), BF16))
                s = jnp.dot(kb, jnp.concatenate(parts, axis=0), preferred_element_type=F32)
                s_car = s[tokens : tokens + 1]
                s = s[:tokens]
                top = jnp.maximum(jnp.max(s, axis=0, keepdims=True), s_car)
                e = jnp.exp((s - top) * scale)
                e_car = jnp.exp((s_car - top) * scale)
                total = jnp.sum(e, axis=0, keepdims=True) + e_car
                o = jnp.dot(v_t[lo : lo + HEAD, :], e.astype(BF16), preferred_element_type=F32)
                o = o + vcar_col[lo : lo + HEAD] * e_car.astype(BF16).astype(F32)
                in_t[lo : lo + HEAD, :] = (o / total + glob_col[lo : lo + HEAD]).astype(BF16)
        inner = in_t[...].T
        upd = jnp.dot(inner, wo_ref[...], preferred_element_type=F32).astype(BF16)
        ybuf[slot] = upd.reshape(npos, rows, WIN * WIN, width)
        for p in window_peers(my_pos, npos) + [my_pos]:
            dst = ci * npos + p

            @pl.when(dst != me)
            def _():
                b_copy(slot, p, dst, me, j).start()

            @pl.when(dst == me)
            def _():
                bl_copy(slot, j).start()

        return carry

    lax.fori_loop(0, own, cube, 0)

    for k, d in enumerate(peers):
        p_copy(k, d, me).wait_send()
    for k, d in enumerate(in_peers):
        c_copy(k, d, ii).wait_send()
    for j in range(span):
        for k, d in enumerate(peers):
            f_copy(k, j, d, me).wait_send()
    for j in range(span):
        for d in peers:
            b_copy(0, 0, me, d, j).wait_recv()
        bl_copy(my_ci * span + j, j).wait()
    for slot in range(own):
        for p in range(npos):
            dst = (slot // span) * npos + p

            @pl.when(dst != me)
            def _():
                b_copy(slot, p, dst, me, slot % span).wait_send()


def body(n_in, n_win, tokens, w, w_out):
    rows, xl, dep, width = tokens.shape
    strips = xl // WIN
    npos = WIN // rows
    span = strips // n_win
    own = span * (n_win // npos)
    group_cars = (n_win // npos) * strips
    cube = WIN * WIN * WIN
    block = (rows, WIN * WIN, width)
    hbm = pl.BlockSpec(memory_space=pl.ANY)
    dma = pltpu.SemaphoreType.DMA
    shaped = tokens.reshape(rows, strips, WIN * dep, width)
    out = pl.pallas_call(
        functools.partial(kernel, n_in, n_win, rows, strips),
        out_shape=jax.ShapeDtypeStruct(shaped.shape, BF16),
        in_specs=[hbm, hbm, hbm],
        out_specs=hbm,
        scratch_shapes=[
            pltpu.VMEM((strips,) + block, BF16),
            pltpu.VMEM(w.shape, BF16),
            pltpu.VMEM(w_out.shape, BF16),
            pltpu.VMEM((strips,) + block, BF16),
            pltpu.VMEM((own, npos) + block, BF16),
            pltpu.VMEM((own, npos) + block, BF16),
            pltpu.VMEM((n_win, strips, width), F32),
            pltpu.VMEM((n_in, group_cars, width), BF16),
            pltpu.VMEM((width, width), BF16),
            pltpu.VMEM((width, width), BF16),
            pltpu.VMEM((cube + 16, width), BF16),
            pltpu.VMEM((width, cube), BF16),
            pltpu.VMEM((width, cube), BF16),
            pltpu.VMEM((width, cube), BF16),
            pltpu.VMEM((group_cars, width), F32),
            pltpu.VMEM((group_cars, width), F32),
            pltpu.VMEM((group_cars, width), F32),
            dma((n_win, span)),
            dma((n_win, span)),
            dma((own, npos)),
            dma((n_win, span)),
            dma((n_win,)),
            dma((n_win,)),
            dma((n_in,)),
            dma((n_in,)),
            dma((span,)),
            dma((span,)),
            dma((strips,)),
            dma((2,)),
        ],
        compiler_params=pltpu.CompilerParams(
            collective_id=0, has_side_effects=True, vmem_limit_bytes=56 * 1024 * 1024
        ),
        cost_estimate=pl.CostEstimate(
            flops=2 * own * cube * width * (4 * width + 2 * cube),
            bytes_accessed=4 * own * cube * width,
            transcendentals=own * FOCUS_GROUPS * cube * cube,
        ),
    )(shaped, w, w_out)
    return out.reshape(tokens.shape)


def solution(mesh):
    return jax.shard_map(
        functools.partial(body, mesh.shape["inline"], mesh.shape["window"]),
        mesh=mesh,
        in_specs=(P(("replica", "inline", "window"), None, None, None), P(), P()),
        out_specs=P(("replica", "inline", "window"), None, None, None),
        check_vma=False,
    )
```

```python
import functools

import jax
import jax.numpy as jnp
from jax import lax
from jax.experimental import pallas as pl
from jax.experimental.pallas import tpu as pltpu
from jax.sharding import PartitionSpec as P

EMBED_SPAN = 512
FOCUS_GROUPS = 16
HEAD = EMBED_SPAN // FOCUS_GROUPS
WIN = 8
EPSILON = 1e-05
LOG2_E = 1.4426950408889634
MESH = pl.DeviceIdType.MESH
F32 = jnp.float32
BF16 = jnp.bfloat16


def standardize(x):
    center = x - jnp.mean(x, axis=-1, keepdims=True)
    spread = jnp.mean(center * center, axis=-1, keepdims=True)
    return center * lax.rsqrt(spread + EPSILON)


def window_peers(me, n):
    if n % 2:
        return [lax.rem(me + o, n) for o in range(1, n)]
    same = [lax.rem(me + o, n) for o in range(2, n, 2)]
    odd = [lax.rem(n + c - me, n) for c in range(n - 1, 0, -2)]
    return same + odd


def kernel(
    n_in, n_win, rows, strips,
    tok_ref, w_hbm, wo_hbm, out_ref,
    tok_buf, w_ref, wo_ref,
    normed, xin, ybuf, psum, cars, wq_t, wv_t, k_buf, q_t, v_t, in_t, glob_buf, kcar_buf, vcar_buf,
    fsend, frecv, bsend, brecv, psend, precv, csend, crecv, lsem, blsem, tsem, wsem,
):
    ii = lax.axis_index("inline")
    me = lax.axis_index("window")
    span = strips // n_win
    npos = WIN // rows
    n_ci = n_win // npos
    own = span * n_ci
    group_cars = n_ci * strips
    width = EMBED_SPAN
    tokens = WIN * WIN * WIN
    my_ci = me // npos
    my_pos = lax.rem(me, npos)
    peers = window_peers(me, n_win)
    in_peers = [lax.rem(ii + o, n_in) for o in range(1, n_in)]

    barrier = pltpu.get_barrier_semaphore()
    for d in peers:
        pl.semaphore_signal(barrier, inc=1, device_id={"window": d}, device_id_type=MESH)
    for d in in_peers:
        pl.semaphore_signal(barrier, inc=1, device_id={"inline": d}, device_id_type=MESH)

    order = [(j, k, d) for j in range(span) for k, d in enumerate(peers + [me])]

    def t_copy(n):
        j, _, d = order[n]
        return pltpu.make_async_copy(tok_ref.at[:, d * span + j], tok_buf.at[n], tsem.at[n])

    for n in range(len(order)):
        t_copy(n).start()
    w_copy = pltpu.make_async_copy(w_hbm, w_ref, wsem.at[0])
    wo_copy = pltpu.make_async_copy(wo_hbm, wo_ref, wsem.at[1])
    w_copy.start()
    wo_copy.start()

    def p_copy(k, d, src):
        return pltpu.make_async_remote_copy(
            src_ref=psum.at[src], dst_ref=psum.at[src], send_sem=psend.at[k], recv_sem=precv.at[src],
            device_id={"window": d}, device_id_type=MESH,
        )

    def f_copy(k, j, d, src):
        return pltpu.make_async_remote_copy(
            src_ref=normed.at[d * span + j], dst_ref=xin.at[(src // npos) * span + j, lax.rem(src, npos)],
            send_sem=fsend.at[k, j], recv_sem=frecv.at[src, j],
            device_id={"window": d}, device_id_type=MESH,
        )

    def l_copy(j):
        return pltpu.make_async_copy(
            normed.at[me * span + j], xin.at[my_ci * span + j, my_pos], lsem.at[j]
        )

    for n, (j, k, d) in enumerate(order):
        t_copy(n).wait()
        x = standardize(tok_buf[n].astype(F32)).astype(BF16)
        normed[d * span + j] = x
        psum[me, pl.ds(d * span + j, 1), :] = jnp.sum(x.astype(F32), axis=(0, 1))[None, :]
        if n == 0:
            pl.semaphore_wait(barrier, len(peers) + len(in_peers))
        if j == 0:
            if k == len(peers):
                l_copy(j).start()
            else:
                f_copy(k, j, d, me).start()
    for k, d in enumerate(peers):
        p_copy(k, d, me).start()
    for j, k, d in order:
        if j:
            if k == len(peers):
                l_copy(j).start()
            else:
                f_copy(k, j, d, me).start()
    w_copy.wait()
    wo_copy.wait()

    wq_t[...] = w_ref[:, :width].T
    wv_t[...] = w_ref[:, 2 * width :].T

    for d in peers:
        p_copy(0, d, d).wait_recv()
    for ci in range(n_ci):
        total = psum[ci * npos]
        for p in range(1, npos):
            total = total + psum[ci * npos + p]
        cars[ii, pl.ds(ci * strips, strips), :] = standardize(total * (1.0 / tokens)).astype(BF16)

    def c_copy(k, d, src):
        return pltpu.make_async_remote_copy(
            src_ref=cars.at[src], dst_ref=cars.at[src], send_sem=csend.at[k], recv_sem=crecv.at[src],
            device_id={"inline": d}, device_id_type=MESH,
        )

    for k, d in enumerate(in_peers):
        c_copy(k, d, ii).start()

    scale = HEAD ** (-0.5)
    sharp = scale * LOG2_E
    mine = jnp.dot(cars[ii], w_ref[...], preferred_element_type=F32).astype(BF16)
    kcar_buf[...] = mine[:, width : 2 * width].astype(F32)
    vcar_buf[...] = mine[:, 2 * width :].astype(F32)
    for d in in_peers:
        c_copy(0, d, d).wait_recv()
    every = cars[...].reshape(n_in * group_cars, width)
    kv = jnp.dot(every, w_ref[:, width:], preferred_element_type=F32).astype(BF16)
    col_head = lax.broadcasted_iota(jnp.int32, (group_cars, width), 1) // HEAD
    q_car = mine[:, :width].astype(F32)
    glob = jnp.zeros((group_cars, width), F32)
    for h in range(FOCUS_GROUPS):
        q_h = jnp.where(col_head == h, q_car, 0.0).astype(BF16)
        s = lax.dot_general(q_h, kv[:, :width], (((1,), (1,)), ((), ())), preferred_element_type=F32) * scale
        e = jnp.exp(s - jnp.max(s, axis=-1, keepdims=True))
        t = jnp.sum(e, axis=-1, keepdims=True)
        o = jnp.dot(e.astype(BF16), kv[:, width:], preferred_element_type=F32) / t
        glob = jnp.where(col_head == h, o, glob)
    glob_buf[...] = glob

    def b_copy(slot, p, dst, owner, j):
        return pltpu.make_async_remote_copy(
            src_ref=ybuf.at[slot, p], dst_ref=out_ref.at[:, owner * span + j],
            send_sem=bsend.at[slot, p], recv_sem=brecv.at[owner, j],
            device_id={"window": dst}, device_id_type=MESH,
        )

    def bl_copy(slot, j):
        return pltpu.make_async_copy(ybuf.at[slot, my_pos], out_ref.at[:, me * span + j], blsem.at[j])

    def cube(slot, carry):
        ci = slot // span
        j = lax.rem(slot, span)
        for p in range(npos):
            src = ci * npos + p

            @pl.when(src != me)
            def _():
                f_copy(0, j, me, src).wait_recv()

            @pl.when(src == me)
            def _():
                l_copy(j).wait()

        x = xin[slot].reshape(tokens, width)
        row = ci * strips + me * span + j
        pick = lax.broadcasted_iota(jnp.int32, (group_cars, width), 0) == row

        def chosen(ref):
            return jnp.sum(jnp.where(pick, ref[...], 0.0), axis=0, keepdims=True)

        def column(r):
            return jnp.broadcast_to(r, (128, width)).T[:, :1]

        k_buf[:tokens, :] = jnp.dot(x, w_ref[:, width : 2 * width], preferred_element_type=F32).astype(BF16)
        k_buf[tokens:, :] = jnp.broadcast_to(chosen(kcar_buf), (16, width)).astype(BF16)
        nt = (((1,), (1,)), ((), ()))
        q_t[...] = lax.dot_general(wq_t[...], x, nt, preferred_element_type=F32).astype(BF16)
        v_t[...] = lax.dot_general(wv_t[...], x, nt, preferred_element_type=F32).astype(BF16)
        glob_col = column(chosen(glob_buf))
        vcar_col = column(chosen(vcar_buf))
        for hb in range(width // 128):
            kb = k_buf[:, hb * 128 : (hb + 1) * 128]
            for h4 in range(128 // HEAD):
                lo = hb * 128 + h4 * HEAD
                parts = [q_t[lo : lo + HEAD, :]]
                if h4:
                    parts.insert(0, jnp.zeros((h4 * HEAD, tokens), BF16))
                if h4 < 128 // HEAD - 1:
                    parts.append(jnp.zeros((128 - (h4 + 1) * HEAD, tokens), BF16))
                s = jnp.dot(kb, jnp.concatenate(parts, axis=0), preferred_element_type=F32)
                s_car = s[tokens : tokens + 1]
                s = s[:tokens]
                top = jnp.maximum(jnp.max(s, axis=0, keepdims=True), s_car)
                e = jnp.exp2((s - top) * sharp)
                e_car = jnp.exp2((s_car - top) * sharp)
                total = jnp.sum(e, axis=0, keepdims=True) + e_car
                o = jnp.dot(v_t[lo : lo + HEAD, :], e.astype(BF16), preferred_element_type=F32)
                o = o + vcar_col[lo : lo + HEAD] * e_car.astype(BF16).astype(F32)
                in_t[lo : lo + HEAD, :] = (o / total + glob_col[lo : lo + HEAD]).astype(BF16)
        inner = in_t[...].T
        upd = jnp.dot(inner, wo_ref[...], preferred_element_type=F32).astype(BF16)
        ybuf[slot] = upd.reshape(npos, rows, WIN * WIN, width)
        for p in window_peers(my_pos, npos) + [my_pos]:
            dst = ci * npos + p

            @pl.when(dst != me)
            def _():
                b_copy(slot, p, dst, me, j).start()

            @pl.when(dst == me)
            def _():
                bl_copy(slot, j).start()

        return carry

    lax.fori_loop(0, own, cube, 0)

    for k, d in enumerate(peers):
        p_copy(k, d, me).wait_send()
    for k, d in enumerate(in_peers):
        c_copy(k, d, ii).wait_send()
    for j in range(span):
        for k, d in enumerate(peers):
            f_copy(k, j, d, me).wait_send()
    for j in range(span):
        for d in peers:
            b_copy(0, 0, me, d, j).wait_recv()
        bl_copy(my_ci * span + j, j).wait()
    for slot in range(own):
        for p in range(npos):
            dst = (slot // span) * npos + p

            @pl.when(dst != me)
            def _():
                b_copy(slot, p, dst, me, slot % span).wait_send()


def body(n_in, n_win, tokens, w, w_out):
    rows, xl, dep, width = tokens.shape
    strips = xl // WIN
    npos = WIN // rows
    span = strips // n_win
    own = span * (n_win // npos)
    group_cars = (n_win // npos) * strips
    cube = WIN * WIN * WIN
    block = (rows, WIN * WIN, width)
    hbm = pl.BlockSpec(memory_space=pl.ANY)
    dma = pltpu.SemaphoreType.DMA
    shaped = tokens.reshape(rows, strips, WIN * dep, width)
    out = pl.pallas_call(
        functools.partial(kernel, n_in, n_win, rows, strips),
        out_shape=jax.ShapeDtypeStruct(shaped.shape, BF16),
        in_specs=[hbm, hbm, hbm],
        out_specs=pl.BlockSpec(memory_space=pl.ANY),
        scratch_shapes=[
            pltpu.VMEM((strips,) + block, BF16),
            pltpu.VMEM(w.shape, BF16),
            pltpu.VMEM(w_out.shape, BF16),
            pltpu.VMEM((strips,) + block, BF16),
            pltpu.VMEM((own, npos) + block, BF16),
            pltpu.VMEM((own, npos) + block, BF16),
            pltpu.VMEM((n_win, strips, width), F32),
            pltpu.VMEM((n_in, group_cars, width), BF16),
            pltpu.VMEM((width, width), BF16),
            pltpu.VMEM((width, width), BF16),
            pltpu.VMEM((cube + 16, width), BF16),
            pltpu.VMEM((width, cube), BF16),
            pltpu.VMEM((width, cube), BF16),
            pltpu.VMEM((width, cube), BF16),
            pltpu.VMEM((group_cars, width), F32),
            pltpu.VMEM((group_cars, width), F32),
            pltpu.VMEM((group_cars, width), F32),
            dma((n_win, span)),
            dma((n_win, span)),
            dma((own, npos)),
            dma((n_win, span)),
            dma((n_win,)),
            dma((n_win,)),
            dma((n_in,)),
            dma((n_in,)),
            dma((span,)),
            dma((span,)),
            dma((strips,)),
            dma((2,)),
        ],
        compiler_params=pltpu.CompilerParams(
            collective_id=0, has_side_effects=True, vmem_limit_bytes=36 * 1024 * 1024
        ),
        cost_estimate=pl.CostEstimate(
            flops=2 * own * cube * width * (4 * width + 2 * cube),
            bytes_accessed=4 * own * cube * width,
            transcendentals=own * FOCUS_GROUPS * cube * cube,
        ),
    )(*(pltpu.with_memory_space_constraint(a, pltpu.HBM) for a in (shaped, w, w_out)))
    return out.reshape(tokens.shape)


def solution(mesh):
    return jax.shard_map(
        functools.partial(body, mesh.shape["inline"], mesh.shape["window"]),
        mesh=mesh,
        in_specs=(P(("replica", "inline", "window"), None, None, None), P(), P()),
        out_specs=P(("replica", "inline", "window"), None, None, None),
        check_vma=False,
    )
```

```python
import functools

import jax
import jax.numpy as jnp
from jax import lax
from jax.experimental import pallas as pl
from jax.experimental.pallas import tpu as pltpu
from jax.sharding import PartitionSpec as P

EMBED_SPAN = 512
FOCUS_GROUPS = 16
HEAD = EMBED_SPAN // FOCUS_GROUPS
WIN = 8
EPSILON = 1e-05
LOG2_E = 1.4426950408889634
MESH = pl.DeviceIdType.MESH
F32 = jnp.float32
BF16 = jnp.bfloat16


def standardize(x):
    center = x - jnp.mean(x, axis=-1, keepdims=True)
    spread = jnp.mean(center * center, axis=-1, keepdims=True)
    return center * lax.rsqrt(spread + EPSILON)


def window_peers(me, n):
    if n % 2:
        return [lax.rem(me + o, n) for o in range(1, n)]
    same = [lax.rem(me + o, n) for o in range(2, n, 2)]
    odd = [lax.rem(n + c - me, n) for c in range(n - 1, 0, -2)]
    return same + odd


def kernel(
    n_in, n_win, rows, strips,
    tok_ref, w_hbm, wo_hbm, out_ref,
    tok_buf, w_ref, wo_ref,
    normed, xin, ybuf, psum, cars, wq_t, wv_t, k_buf, q_t, v_t, in_t, glob_buf, qcar_buf, kcar_buf, vcar_buf,
    fsend, frecv, bsend, brecv, psend, precv, csend, crecv, lsem, blsem, tsem, wsem,
):
    ii = lax.axis_index("inline")
    me = lax.axis_index("window")
    span = strips // n_win
    npos = WIN // rows
    n_ci = n_win // npos
    own = span * n_ci
    group_cars = n_ci * strips
    width = EMBED_SPAN
    tokens = WIN * WIN * WIN
    my_ci = me // npos
    my_pos = lax.rem(me, npos)
    peers = window_peers(me, n_win)
    in_peers = [lax.rem(ii + o, n_in) for o in range(1, n_in)]

    barrier = pltpu.get_barrier_semaphore()
    for d in peers:
        pl.semaphore_signal(barrier, inc=1, device_id={"window": d}, device_id_type=MESH)
    for d in in_peers:
        pl.semaphore_signal(barrier, inc=1, device_id={"inline": d}, device_id_type=MESH)

    order = [(j, k, d) for j in range(span) for k, d in enumerate(peers + [me])]

    def t_copy(n):
        j, _, d = order[n]
        return pltpu.make_async_copy(tok_ref.at[:, d * span + j], tok_buf.at[n], tsem.at[n])

    for n in range(len(order)):
        t_copy(n).start()
    w_copy = pltpu.make_async_copy(w_hbm, w_ref, wsem.at[0])
    wo_copy = pltpu.make_async_copy(wo_hbm, wo_ref, wsem.at[1])
    w_copy.start()
    wo_copy.start()

    def p_copy(k, d, src):
        return pltpu.make_async_remote_copy(
            src_ref=psum.at[src], dst_ref=psum.at[src], send_sem=psend.at[k], recv_sem=precv.at[src],
            device_id={"window": d}, device_id_type=MESH,
        )

    def f_copy(k, j, d, src):
        return pltpu.make_async_remote_copy(
            src_ref=normed.at[d * span + j], dst_ref=xin.at[(src // npos) * span + j, lax.rem(src, npos)],
            send_sem=fsend.at[k, j], recv_sem=frecv.at[src, j],
            device_id={"window": d}, device_id_type=MESH,
        )

    def l_copy(j):
        return pltpu.make_async_copy(
            normed.at[me * span + j], xin.at[my_ci * span + j, my_pos], lsem.at[j]
        )

    for n, (j, k, d) in enumerate(order):
        t_copy(n).wait()
        x = standardize(tok_buf[n].astype(F32)).astype(BF16)
        normed[d * span + j] = x
        psum[me, pl.ds(d * span + j, 1), :] = jnp.sum(x.astype(F32), axis=(0, 1))[None, :]
        if n == 0:
            pl.semaphore_wait(barrier, len(peers) + len(in_peers))
        if j == 0:
            if k == len(peers):
                l_copy(j).start()
            else:
                f_copy(k, j, d, me).start()
    for k, d in enumerate(peers):
        p_copy(k, d, me).start()
    for j, k, d in order:
        if j:
            if k == len(peers):
                l_copy(j).start()
            else:
                f_copy(k, j, d, me).start()
    w_copy.wait()
    wo_copy.wait()

    wq_t[...] = w_ref[:, :width].T
    wv_t[...] = w_ref[:, 2 * width :].T

    for d in peers:
        p_copy(0, d, d).wait_recv()
    for ci in range(n_ci):
        total = psum[ci * npos]
        for p in range(1, npos):
            total = total + psum[ci * npos + p]
        cars[ii, pl.ds(ci * strips, strips), :] = standardize(total * (1.0 / tokens)).astype(BF16)

    def c_copy(k, d, src):
        return pltpu.make_async_remote_copy(
            src_ref=cars.at[src], dst_ref=cars.at[src], send_sem=csend.at[k], recv_sem=crecv.at[src],
            device_id={"inline": d}, device_id_type=MESH,
        )

    for k, d in enumerate(in_peers):
        c_copy(k, d, ii).start()

    scale = HEAD ** (-0.5)
    sharp = scale * LOG2_E
    mine = jnp.dot(cars[ii], w_ref[...], preferred_element_type=F32).astype(BF16)
    kcar_buf[...] = mine[:, width : 2 * width].astype(F32)
    vcar_buf[...] = mine[:, 2 * width :].astype(F32)
    qcar_buf[...] = mine[:, :width].astype(F32)

    def global_part():
        for d in in_peers:
            c_copy(0, d, d).wait_recv()
        every = cars[...].reshape(n_in * group_cars, width)
        kv = jnp.dot(every, w_ref[:, width:], preferred_element_type=F32).astype(BF16)
        col_head = lax.broadcasted_iota(jnp.int32, (group_cars, width), 1) // HEAD
        q_car = qcar_buf[...]
        glob = jnp.zeros((group_cars, width), F32)
        for h in range(FOCUS_GROUPS):
            q_h = jnp.where(col_head == h, q_car, 0.0).astype(BF16)
            s = lax.dot_general(q_h, kv[:, :width], (((1,), (1,)), ((), ())), preferred_element_type=F32) * scale
            e = jnp.exp(s - jnp.max(s, axis=-1, keepdims=True))
            t = jnp.sum(e, axis=-1, keepdims=True)
            o = jnp.dot(e.astype(BF16), kv[:, width:], preferred_element_type=F32) / t
            glob = jnp.where(col_head == h, o, glob)
        glob_buf[...] = glob

    def b_copy(slot, p, dst, owner, j):
        return pltpu.make_async_remote_copy(
            src_ref=ybuf.at[slot, p], dst_ref=out_ref.at[:, owner * span + j],
            send_sem=bsend.at[slot, p], recv_sem=brecv.at[owner, j],
            device_id={"window": dst}, device_id_type=MESH,
        )

    def bl_copy(slot, j):
        return pltpu.make_async_copy(ybuf.at[slot, my_pos], out_ref.at[:, me * span + j], blsem.at[j])

    halves = 2 if npos % 2 == 0 else 1
    per = npos // halves
    queries = tokens // halves

    def half_cube(it, carry):
        slot = it // halves
        ci = slot // span
        j = lax.rem(slot, span)
        base = lax.rem(my_pos // per + 1 + lax.rem(it, halves), halves) * per
        row = ci * strips + me * span + j
        pick = lax.broadcasted_iota(jnp.int32, (group_cars, width), 0) == row
        nt = (((1,), (1,)), ((), ()))

        def chosen(ref):
            return jnp.sum(jnp.where(pick, ref[...], 0.0), axis=0, keepdims=True)

        def column(r):
            return jnp.broadcast_to(r, (128, width)).T[:, :1]

        @pl.when(lax.rem(it, halves) == 0)
        def _():
            for p in range(npos):
                src = ci * npos + p

                @pl.when(src != me)
                def _():
                    f_copy(0, j, me, src).wait_recv()

                @pl.when(src == me)
                def _():
                    l_copy(j).wait()

            x = xin[slot].reshape(tokens, width)
            k_buf[:tokens, :] = jnp.dot(x, w_ref[:, width : 2 * width], preferred_element_type=F32).astype(BF16)
            k_buf[tokens:, :] = jnp.broadcast_to(chosen(kcar_buf), (16, width)).astype(BF16)
            v_t[...] = lax.dot_general(wv_t[...], x, nt, preferred_element_type=F32).astype(BF16)

        x_half = xin[slot, pl.ds(base, per)].reshape(queries, width)
        q_t[...] = lax.dot_general(wq_t[...], x_half, nt, preferred_element_type=F32).astype(BF16)
        vcar_col = column(chosen(vcar_buf))
        for hb in range(width // 128):
            kb = k_buf[:, hb * 128 : (hb + 1) * 128]
            for h4 in range(128 // HEAD):
                lo = hb * 128 + h4 * HEAD
                parts = [q_t[lo : lo + HEAD, :]]
                if h4:
                    parts.insert(0, jnp.zeros((h4 * HEAD, queries), BF16))
                if h4 < 128 // HEAD - 1:
                    parts.append(jnp.zeros((128 - (h4 + 1) * HEAD, queries), BF16))
                s = jnp.dot(kb, jnp.concatenate(parts, axis=0), preferred_element_type=F32)
                s_car = s[tokens : tokens + 1]
                s = s[:tokens]
                top = jnp.maximum(jnp.max(s, axis=0, keepdims=True), s_car)
                e = jnp.exp2((s - top) * sharp)
                e_car = jnp.exp2((s_car - top) * sharp)
                total = jnp.sum(e, axis=0, keepdims=True) + e_car
                o = jnp.dot(v_t[lo : lo + HEAD, :], e.astype(BF16), preferred_element_type=F32)
                o = o + vcar_col[lo : lo + HEAD] * e_car.astype(BF16).astype(F32)
                in_t[lo : lo + HEAD, :] = o / total

        pl.when(it == 0)(global_part)
        inner = (in_t[...] + column(chosen(glob_buf))).astype(BF16).T
        upd = jnp.dot(inner, wo_ref[...], preferred_element_type=F32).astype(BF16)
        ybuf[slot, pl.ds(base, per)] = upd.reshape(per, rows, WIN * WIN, width)
        for o in range(per):
            p = base + o
            dst = ci * npos + p

            @pl.when(dst != me)
            def _():
                b_copy(slot, p, dst, me, j).start()

            @pl.when(dst == me)
            def _():
                bl_copy(slot, j).start()

        return carry

    lax.fori_loop(0, own * halves, half_cube, 0)

    for k, d in enumerate(peers):
        p_copy(k, d, me).wait_send()
    for k, d in enumerate(in_peers):
        c_copy(k, d, ii).wait_send()
    for j in range(span):
        for k, d in enumerate(peers):
            f_copy(k, j, d, me).wait_send()
    for j in range(span):
        for d in peers:
            b_copy(0, 0, me, d, j).wait_recv()
        bl_copy(my_ci * span + j, j).wait()
    for slot in range(own):
        for p in range(npos):
            dst = (slot // span) * npos + p

            @pl.when(dst != me)
            def _():
                b_copy(slot, p, dst, me, slot % span).wait_send()


def body(n_in, n_win, tokens, w, w_out):
    rows, xl, dep, width = tokens.shape
    strips = xl // WIN
    npos = WIN // rows
    span = strips // n_win
    own = span * (n_win // npos)
    group_cars = (n_win // npos) * strips
    cube = WIN * WIN * WIN
    queries = cube // 2 if npos % 2 == 0 else cube
    block = (rows, WIN * WIN, width)
    hbm = pl.BlockSpec(memory_space=pl.ANY)
    dma = pltpu.SemaphoreType.DMA
    shaped = tokens.reshape(rows, strips, WIN * dep, width)
    out = pl.pallas_call(
        functools.partial(kernel, n_in, n_win, rows, strips),
        out_shape=jax.ShapeDtypeStruct(shaped.shape, BF16),
        in_specs=[hbm, hbm, hbm],
        out_specs=pl.BlockSpec(memory_space=pl.ANY),
        scratch_shapes=[
            pltpu.VMEM((strips,) + block, BF16),
            pltpu.VMEM(w.shape, BF16),
            pltpu.VMEM(w_out.shape, BF16),
            pltpu.VMEM((strips,) + block, BF16),
            pltpu.VMEM((own, npos) + block, BF16),
            pltpu.VMEM((own, npos) + block, BF16),
            pltpu.VMEM((n_win, strips, width), F32),
            pltpu.VMEM((n_in, group_cars, width), BF16),
            pltpu.VMEM((width, width), BF16),
            pltpu.VMEM((width, width), BF16),
            pltpu.VMEM((cube + 16, width), BF16),
            pltpu.VMEM((width, queries), BF16),
            pltpu.VMEM((width, cube), BF16),
            pltpu.VMEM((width, queries), F32),
            pltpu.VMEM((group_cars, width), F32),
            pltpu.VMEM((group_cars, width), F32),
            pltpu.VMEM((group_cars, width), F32),
            pltpu.VMEM((group_cars, width), F32),
            dma((n_win, span)),
            dma((n_win, span)),
            dma((own, npos)),
            dma((n_win, span)),
            dma((n_win,)),
            dma((n_win,)),
            dma((n_in,)),
            dma((n_in,)),
            dma((span,)),
            dma((span,)),
            dma((strips,)),
            dma((2,)),
        ],
        compiler_params=pltpu.CompilerParams(
            collective_id=0, has_side_effects=True, vmem_limit_bytes=36 * 1024 * 1024
        ),
        cost_estimate=pl.CostEstimate(
            flops=2 * own * cube * width * (4 * width + 2 * cube),
            bytes_accessed=4 * own * cube * width,
            transcendentals=own * FOCUS_GROUPS * cube * cube,
        ),
    )(*(pltpu.with_memory_space_constraint(a, pltpu.HBM) for a in (shaped, w, w_out)))
    return out.reshape(tokens.shape)


def solution(mesh):
    return jax.shard_map(
        functools.partial(body, mesh.shape["inline"], mesh.shape["window"]),
        mesh=mesh,
        in_specs=(P(("replica", "inline", "window"), None, None, None), P(), P()),
        out_specs=P(("replica", "inline", "window"), None, None, None),
        check_vma=False,
    )
```

```python
import functools

import jax
import jax.numpy as jnp
from jax import lax
from jax.experimental import pallas as pl
from jax.experimental.pallas import tpu as pltpu
from jax.sharding import PartitionSpec as P

EMBED_SPAN = 512
FOCUS_GROUPS = 16
HEAD = EMBED_SPAN // FOCUS_GROUPS
WIN = 8
EPSILON = 1e-05
LOG2_E = 1.4426950408889634
MESH = pl.DeviceIdType.MESH
F32 = jnp.float32
BF16 = jnp.bfloat16


def standardize(x):
    center = x - jnp.mean(x, axis=-1, keepdims=True)
    spread = jnp.mean(center * center, axis=-1, keepdims=True)
    return center * lax.rsqrt(spread + EPSILON)


def window_peers(me, n):
    if n % 2:
        return [lax.rem(me + o, n) for o in range(1, n)]
    same = [lax.rem(me + o, n) for o in range(2, n, 2)]
    odd = [lax.rem(n + c - me, n) for c in range(n - 1, 0, -2)]
    return same + odd


def kernel(
    n_in, n_win, rows, strips,
    tok_ref, w_hbm, wo_hbm, out_ref,
    tok_buf, w_ref, wo_ref,
    normed, xin, ybuf, psum, cars, wq_t, wv_t, k_buf, q_t, v_t, in_t, glob_buf, kcar_buf, vcar_buf,
    fsend, frecv, bsend, brecv, psend, precv, csend, crecv, lsem, blsem, tsem, wsem,
):
    ii = lax.axis_index("inline")
    me = lax.axis_index("window")
    span = strips // n_win
    npos = WIN // rows
    n_ci = n_win // npos
    own = span * n_ci
    group_cars = n_ci * strips
    width = EMBED_SPAN
    tokens = WIN * WIN * WIN
    my_ci = me // npos
    my_pos = lax.rem(me, npos)
    peers = window_peers(me, n_win)
    in_peers = [lax.rem(ii + o, n_in) for o in range(1, n_in)]

    barrier = pltpu.get_barrier_semaphore()
    for d in peers:
        pl.semaphore_signal(barrier, inc=1, device_id={"window": d}, device_id_type=MESH)
    for d in in_peers:
        pl.semaphore_signal(barrier, inc=1, device_id={"inline": d}, device_id_type=MESH)

    order = [(j, k, d) for j in range(span) for k, d in enumerate(peers + [me])]

    def t_copy(n):
        j, _, d = order[n]
        return pltpu.make_async_copy(tok_ref.at[:, d * span + j], tok_buf.at[n], tsem.at[n])

    for n in range(len(order)):
        t_copy(n).start()
    w_copy = pltpu.make_async_copy(w_hbm, w_ref, wsem.at[0])
    wo_copy = pltpu.make_async_copy(wo_hbm, wo_ref, wsem.at[1])
    w_copy.start()
    wo_copy.start()

    def p_copy(k, d, src):
        return pltpu.make_async_remote_copy(
            src_ref=psum.at[src], dst_ref=psum.at[src], send_sem=psend.at[k], recv_sem=precv.at[src],
            device_id={"window": d}, device_id_type=MESH,
        )

    def f_copy(k, j, d, src):
        return pltpu.make_async_remote_copy(
            src_ref=normed.at[d * span + j], dst_ref=xin.at[(src // npos) * span + j, lax.rem(src, npos)],
            send_sem=fsend.at[k, j], recv_sem=frecv.at[src, j],
            device_id={"window": d}, device_id_type=MESH,
        )

    def l_copy(j):
        return pltpu.make_async_copy(
            normed.at[me * span + j], xin.at[my_ci * span + j, my_pos], lsem.at[j]
        )

    for n, (j, k, d) in enumerate(order):
        t_copy(n).wait()
        x = standardize(tok_buf[n].astype(F32)).astype(BF16)
        normed[d * span + j] = x
        psum[me, pl.ds(d * span + j, 1), :] = jnp.sum(x.astype(F32), axis=(0, 1))[None, :]
        if n == 0:
            pl.semaphore_wait(barrier, len(peers) + len(in_peers))
        if j == 0:
            if k == len(peers):
                l_copy(j).start()
            else:
                f_copy(k, j, d, me).start()
    for k, d in enumerate(peers):
        p_copy(k, d, me).start()

    def send_round(j):
        for k, d in enumerate(peers):
            f_copy(k, j, d, me).start()
        l_copy(j).start()

    def wait_cube(slot):
        ci = slot // span
        j = lax.rem(slot, span)
        for p in range(npos):
            src = ci * npos + p

            @pl.when(src != me)
            def _():
                f_copy(0, j, me, src).wait_recv()

            @pl.when(src == me)
            def _():
                l_copy(j).wait()

    if span > 1:
        send_round(1)
    w_copy.wait()
    wo_copy.wait()

    wq_t[...] = w_ref[:, :width].T
    wv_t[...] = w_ref[:, 2 * width :].T

    for d in peers:
        p_copy(0, d, d).wait_recv()
    for ci in range(n_ci):
        total = psum[ci * npos]
        for p in range(1, npos):
            total = total + psum[ci * npos + p]
        cars[ii, pl.ds(ci * strips, strips), :] = standardize(total * (1.0 / tokens)).astype(BF16)

    def c_copy(k, d, src):
        return pltpu.make_async_remote_copy(
            src_ref=cars.at[src], dst_ref=cars.at[src], send_sem=csend.at[k], recv_sem=crecv.at[src],
            device_id={"inline": d}, device_id_type=MESH,
        )

    for k, d in enumerate(in_peers):
        c_copy(k, d, ii).start()

    scale = HEAD ** (-0.5)
    sharp = scale * LOG2_E
    mine = jnp.dot(cars[ii], w_ref[...], preferred_element_type=F32).astype(BF16)
    kcar_buf[...] = mine[:, width : 2 * width].astype(F32)
    vcar_buf[...] = mine[:, 2 * width :].astype(F32)
    wait_cube(jnp.int32(0))
    if span > 2:
        send_round(2)
    for d in in_peers:
        c_copy(0, d, d).wait_recv()
    every = cars[...].reshape(n_in * group_cars, width)
    kv = jnp.dot(every, w_ref[:, width:], preferred_element_type=F32).astype(BF16)
    col_head = lax.broadcasted_iota(jnp.int32, (group_cars, width), 1) // HEAD
    q_car = mine[:, :width].astype(F32)
    glob = jnp.zeros((group_cars, width), F32)
    for h in range(FOCUS_GROUPS):
        q_h = jnp.where(col_head == h, q_car, 0.0).astype(BF16)
        s = lax.dot_general(q_h, kv[:, :width], (((1,), (1,)), ((), ())), preferred_element_type=F32) * scale
        e = jnp.exp(s - jnp.max(s, axis=-1, keepdims=True))
        t = jnp.sum(e, axis=-1, keepdims=True)
        o = jnp.dot(e.astype(BF16), kv[:, width:], preferred_element_type=F32) / t
        glob = jnp.where(col_head == h, o, glob)
    glob_buf[...] = glob

    def b_copy(slot, p, dst, owner, j):
        return pltpu.make_async_remote_copy(
            src_ref=ybuf.at[slot, p], dst_ref=out_ref.at[:, owner * span + j],
            send_sem=bsend.at[slot, p], recv_sem=brecv.at[owner, j],
            device_id={"window": dst}, device_id_type=MESH,
        )

    def bl_copy(slot, j):
        return pltpu.make_async_copy(ybuf.at[slot, my_pos], out_ref.at[:, me * span + j], blsem.at[j])

    def cube(slot, carry):
        ci = slot // span
        j = lax.rem(slot, span)
        @pl.when(slot > 0)
        def _():
            wait_cube(slot)

        for later in range(3, span):

            @pl.when(slot == later - 2)
            def _():
                send_round(later)

        x = xin[slot].reshape(tokens, width)
        row = ci * strips + me * span + j
        pick = lax.broadcasted_iota(jnp.int32, (group_cars, width), 0) == row

        def chosen(ref):
            return jnp.sum(jnp.where(pick, ref[...], 0.0), axis=0, keepdims=True)

        def column(r):
            return jnp.broadcast_to(r, (128, width)).T[:, :1]

        k_buf[:tokens, :] = jnp.dot(x, w_ref[:, width : 2 * width], preferred_element_type=F32).astype(BF16)
        k_buf[tokens:, :] = jnp.broadcast_to(chosen(kcar_buf), (16, width)).astype(BF16)
        nt = (((1,), (1,)), ((), ()))
        q_t[...] = lax.dot_general(wq_t[...], x, nt, preferred_element_type=F32).astype(BF16)
        v_t[...] = lax.dot_general(wv_t[...], x, nt, preferred_element_type=F32).astype(BF16)
        glob_col = column(chosen(glob_buf))
        vcar_col = column(chosen(vcar_buf))
        for hb in range(width // 128):
            kb = k_buf[:, hb * 128 : (hb + 1) * 128]
            for h4 in range(128 // HEAD):
                lo = hb * 128 + h4 * HEAD
                parts = [q_t[lo : lo + HEAD, :]]
                if h4:
                    parts.insert(0, jnp.zeros((h4 * HEAD, tokens), BF16))
                if h4 < 128 // HEAD - 1:
                    parts.append(jnp.zeros((128 - (h4 + 1) * HEAD, tokens), BF16))
                s = jnp.dot(kb, jnp.concatenate(parts, axis=0), preferred_element_type=F32)
                s_car = s[tokens : tokens + 1]
                s = s[:tokens]
                top = jnp.maximum(jnp.max(s, axis=0, keepdims=True), s_car)
                e = jnp.exp2((s - top) * sharp)
                e_car = jnp.exp2((s_car - top) * sharp)
                total = jnp.sum(e, axis=0, keepdims=True) + e_car
                o = jnp.dot(v_t[lo : lo + HEAD, :], e.astype(BF16), preferred_element_type=F32)
                o = o + vcar_col[lo : lo + HEAD] * e_car.astype(BF16).astype(F32)
                in_t[lo : lo + HEAD, :] = (o / total + glob_col[lo : lo + HEAD]).astype(BF16)
        inner = in_t[...].T
        upd = jnp.dot(inner, wo_ref[...], preferred_element_type=F32).astype(BF16)
        ybuf[slot] = upd.reshape(npos, rows, WIN * WIN, width)
        for p in window_peers(my_pos, npos) + [my_pos]:
            dst = ci * npos + p

            @pl.when(dst != me)
            def _():
                b_copy(slot, p, dst, me, j).start()

            @pl.when(dst == me)
            def _():
                bl_copy(slot, j).start()

        return carry

    lax.fori_loop(0, own, cube, 0)

    for k, d in enumerate(peers):
        p_copy(k, d, me).wait_send()
    for k, d in enumerate(in_peers):
        c_copy(k, d, ii).wait_send()
    for j in range(span):
        for k, d in enumerate(peers):
            f_copy(k, j, d, me).wait_send()
    for j in range(span):
        for d in peers:
            b_copy(0, 0, me, d, j).wait_recv()
        bl_copy(my_ci * span + j, j).wait()
    for slot in range(own):
        for p in range(npos):
            dst = (slot // span) * npos + p

            @pl.when(dst != me)
            def _():
                b_copy(slot, p, dst, me, slot % span).wait_send()


def body(n_in, n_win, tokens, w, w_out):
    rows, xl, dep, width = tokens.shape
    strips = xl // WIN
    npos = WIN // rows
    span = strips // n_win
    own = span * (n_win // npos)
    group_cars = (n_win // npos) * strips
    cube = WIN * WIN * WIN
    block = (rows, WIN * WIN, width)
    hbm = pl.BlockSpec(memory_space=pl.ANY)
    dma = pltpu.SemaphoreType.DMA
    shaped = tokens.reshape(rows, strips, WIN * dep, width)
    out = pl.pallas_call(
        functools.partial(kernel, n_in, n_win, rows, strips),
        out_shape=jax.ShapeDtypeStruct(shaped.shape, BF16),
        in_specs=[hbm, hbm, hbm],
        out_specs=pl.BlockSpec(memory_space=pl.ANY),
        scratch_shapes=[
            pltpu.VMEM((strips,) + block, BF16),
            pltpu.VMEM(w.shape, BF16),
            pltpu.VMEM(w_out.shape, BF16),
            pltpu.VMEM((strips,) + block, BF16),
            pltpu.VMEM((own, npos) + block, BF16),
            pltpu.VMEM((own, npos) + block, BF16),
            pltpu.VMEM((n_win, strips, width), F32),
            pltpu.VMEM((n_in, group_cars, width), BF16),
            pltpu.VMEM((width, width), BF16),
            pltpu.VMEM((width, width), BF16),
            pltpu.VMEM((cube + 16, width), BF16),
            pltpu.VMEM((width, cube), BF16),
            pltpu.VMEM((width, cube), BF16),
            pltpu.VMEM((width, cube), BF16),
            pltpu.VMEM((group_cars, width), F32),
            pltpu.VMEM((group_cars, width), F32),
            pltpu.VMEM((group_cars, width), F32),
            dma((n_win, span)),
            dma((n_win, span)),
            dma((own, npos)),
            dma((n_win, span)),
            dma((n_win,)),
            dma((n_win,)),
            dma((n_in,)),
            dma((n_in,)),
            dma((span,)),
            dma((span,)),
            dma((strips,)),
            dma((2,)),
        ],
        compiler_params=pltpu.CompilerParams(
            collective_id=0, has_side_effects=True, vmem_limit_bytes=36 * 1024 * 1024
        ),
        cost_estimate=pl.CostEstimate(
            flops=2 * own * cube * width * (4 * width + 2 * cube),
            bytes_accessed=4 * own * cube * width,
            transcendentals=own * FOCUS_GROUPS * cube * cube,
        ),
    )(*(pltpu.with_memory_space_constraint(a, pltpu.HBM) for a in (shaped, w, w_out)))
    return out.reshape(tokens.shape)


def solution(mesh):
    return jax.shard_map(
        functools.partial(body, mesh.shape["inline"], mesh.shape["window"]),
        mesh=mesh,
        in_specs=(P(("replica", "inline", "window"), None, None, None), P(), P()),
        out_specs=P(("replica", "inline", "window"), None, None, None),
        check_vma=False,
    )
```

```python
import functools

import jax
import jax.numpy as jnp
from jax import lax
from jax.experimental import pallas as pl
from jax.experimental.pallas import tpu as pltpu
from jax.sharding import PartitionSpec as P

EMBED_SPAN = 512
FOCUS_GROUPS = 16
HEAD = EMBED_SPAN // FOCUS_GROUPS
WIN = 8
EPSILON = 1e-05
LOG2_E = 1.4426950408889634
MESH = pl.DeviceIdType.MESH
F32 = jnp.float32
BF16 = jnp.bfloat16


def standardize(x):
    center = x - jnp.mean(x, axis=-1, keepdims=True)
    spread = jnp.mean(center * center, axis=-1, keepdims=True)
    return center * lax.rsqrt(spread + EPSILON)


def window_peers(me, n):
    if n % 2:
        return [lax.rem(me + o, n) for o in range(1, n)]
    same = [lax.rem(me + o, n) for o in range(2, n, 2)]
    odd = [lax.rem(n + c - me, n) for c in range(n - 1, 0, -2)]
    return same + odd


def kernel(
    n_in, n_win, rows, strips,
    tok_ref, w_hbm, wo_hbm, out_ref,
    tok_buf, w_ref, wo_ref,
    normed, xin, ybuf, psum, own_cars, all_cars, cars, wq_t, wv_t, k_buf, q_t, v_t, in_t, glob_buf, kcar_buf, vcar_buf,
    fsend, frecv, bsend, brecv, psend, precv, gsend, grecv, csend, crecv, lsem, blsem, tsem, wsem,
):
    ii = lax.axis_index("inline")
    me = lax.axis_index("window")
    span = strips // n_win
    npos = WIN // rows
    n_ci = n_win // npos
    own = span * n_ci
    group_cars = n_ci * strips
    width = EMBED_SPAN
    tokens = WIN * WIN * WIN
    my_ci = me // npos
    my_pos = lax.rem(me, npos)
    peers = window_peers(me, n_win)
    in_peers = [lax.rem(ii + o, n_in) for o in range(1, n_in)]

    barrier = pltpu.get_barrier_semaphore()
    for d in peers:
        pl.semaphore_signal(barrier, inc=1, device_id={"window": d}, device_id_type=MESH)
    for d in in_peers:
        pl.semaphore_signal(barrier, inc=1, device_id={"inline": d}, device_id_type=MESH)

    order = [(j, k, d) for j in range(span) for k, d in enumerate(peers + [me])]

    def t_copy(n):
        j, _, d = order[n]
        return pltpu.make_async_copy(tok_ref.at[:, d * span + j], tok_buf.at[n], tsem.at[n])

    for n in range(len(order)):
        t_copy(n).start()
    w_copy = pltpu.make_async_copy(w_hbm, w_ref, wsem.at[0])
    wo_copy = pltpu.make_async_copy(wo_hbm, wo_ref, wsem.at[1])
    w_copy.start()
    wo_copy.start()

    def p_copy(k, d, src):
        return pltpu.make_async_remote_copy(
            src_ref=psum.at[src, d], dst_ref=psum.at[src, d], send_sem=psend.at[k], recv_sem=precv.at[src],
            device_id={"window": d}, device_id_type=MESH,
        )

    def f_copy(k, j, d, src):
        return pltpu.make_async_remote_copy(
            src_ref=normed.at[d * span + j], dst_ref=xin.at[(src // npos) * span + j, lax.rem(src, npos)],
            send_sem=fsend.at[k, j], recv_sem=frecv.at[src, j],
            device_id={"window": d}, device_id_type=MESH,
        )

    def l_copy(j):
        return pltpu.make_async_copy(
            normed.at[me * span + j], xin.at[my_ci * span + j, my_pos], lsem.at[j]
        )

    for n, (j, k, d) in enumerate(order):
        t_copy(n).wait()
        x = standardize(tok_buf[n].astype(F32)).astype(BF16)
        normed[d * span + j] = x
        psum[me, d, pl.ds(j, 1), :] = jnp.sum(x.astype(F32), axis=(0, 1))[None, :]
        if n == 0:
            pl.semaphore_wait(barrier, len(peers) + len(in_peers))
        if j == 0:
            if k == len(peers):
                l_copy(j).start()
            else:
                f_copy(k, j, d, me).start()
    for k, d in enumerate(peers):
        p_copy(k, d, me).start()

    def send_round(j):
        for k, d in enumerate(peers):
            f_copy(k, j, d, me).start()
        l_copy(j).start()

    if span > 1:
        send_round(1)
    w_copy.wait()
    wo_copy.wait()

    wq_t[...] = w_ref[:, :width].T
    wv_t[...] = w_ref[:, 2 * width :].T

    def g_copy(k, d, src):
        return pltpu.make_async_remote_copy(
            src_ref=own_cars.at[src], dst_ref=own_cars.at[src], send_sem=gsend.at[k], recv_sem=grecv.at[src],
            device_id={"window": d}, device_id_type=MESH,
        )

    for d in peers:
        p_copy(0, me, d).wait_recv()
    for ci in range(n_ci):
        total = psum[ci * npos, me]
        for p in range(1, npos):
            total = total + psum[ci * npos + p, me]
        own_cars[me, ci] = standardize(total * (1.0 / tokens))
    for k, d in enumerate(peers):
        g_copy(k, d, me).start()
    for j in range(2, span):
        send_round(j)
    for d in peers:
        g_copy(0, me, d).wait_recv()
    for ci in range(n_ci):
        for w in range(n_win):
            first = ci * strips + w * span
            all_cars[first : first + span, :] = own_cars[w, ci]
    cars[ii] = all_cars[...].astype(BF16)

    def c_copy(k, d, src):
        return pltpu.make_async_remote_copy(
            src_ref=cars.at[src], dst_ref=cars.at[src], send_sem=csend.at[k], recv_sem=crecv.at[src],
            device_id={"inline": d}, device_id_type=MESH,
        )

    for k, d in enumerate(in_peers):
        c_copy(k, d, ii).start()

    scale = HEAD ** (-0.5)
    sharp = scale * LOG2_E
    mine = jnp.dot(cars[ii], w_ref[...], preferred_element_type=F32).astype(BF16)
    kcar_buf[...] = mine[:, width : 2 * width].astype(F32)
    vcar_buf[...] = mine[:, 2 * width :].astype(F32)
    for d in in_peers:
        c_copy(0, d, d).wait_recv()
    every = cars[...].reshape(n_in * group_cars, width)
    kv = jnp.dot(every, w_ref[:, width:], preferred_element_type=F32).astype(BF16)
    col_head = lax.broadcasted_iota(jnp.int32, (group_cars, width), 1) // HEAD
    q_car = mine[:, :width].astype(F32)
    glob = jnp.zeros((group_cars, width), F32)
    for h in range(FOCUS_GROUPS):
        q_h = jnp.where(col_head == h, q_car, 0.0).astype(BF16)
        s = lax.dot_general(q_h, kv[:, :width], (((1,), (1,)), ((), ())), preferred_element_type=F32) * scale
        e = jnp.exp(s - jnp.max(s, axis=-1, keepdims=True))
        t = jnp.sum(e, axis=-1, keepdims=True)
        o = jnp.dot(e.astype(BF16), kv[:, width:], preferred_element_type=F32) / t
        glob = jnp.where(col_head == h, o, glob)
    glob_buf[...] = glob

    def b_copy(slot, p, dst, owner, j):
        return pltpu.make_async_remote_copy(
            src_ref=ybuf.at[slot, p], dst_ref=out_ref.at[:, owner * span + j],
            send_sem=bsend.at[slot, p], recv_sem=brecv.at[owner, j],
            device_id={"window": dst}, device_id_type=MESH,
        )

    def bl_copy(slot, j):
        return pltpu.make_async_copy(ybuf.at[slot, my_pos], out_ref.at[:, me * span + j], blsem.at[j])

    def cube(slot, carry):
        ci = slot // span
        j = lax.rem(slot, span)
        for p in range(npos):
            src = ci * npos + p

            @pl.when(src != me)
            def _():
                f_copy(0, j, me, src).wait_recv()

            @pl.when(src == me)
            def _():
                l_copy(j).wait()

        x = xin[slot].reshape(tokens, width)
        row = ci * strips + me * span + j
        pick = lax.broadcasted_iota(jnp.int32, (group_cars, width), 0) == row

        def chosen(ref):
            return jnp.sum(jnp.where(pick, ref[...], 0.0), axis=0, keepdims=True)

        def column(r):
            return jnp.broadcast_to(r, (128, width)).T[:, :1]

        k_buf[:tokens, :] = jnp.dot(x, w_ref[:, width : 2 * width], preferred_element_type=F32).astype(BF16)
        k_buf[tokens:, :] = jnp.broadcast_to(chosen(kcar_buf), (16, width)).astype(BF16)
        nt = (((1,), (1,)), ((), ()))
        q_t[...] = lax.dot_general(wq_t[...], x, nt, preferred_element_type=F32).astype(BF16)
        v_t[...] = lax.dot_general(wv_t[...], x, nt, preferred_element_type=F32).astype(BF16)
        glob_col = column(chosen(glob_buf))
        vcar_col = column(chosen(vcar_buf))
        for hb in range(width // 128):
            kb = k_buf[:, hb * 128 : (hb + 1) * 128]
            for h4 in range(128 // HEAD):
                lo = hb * 128 + h4 * HEAD
                parts = [q_t[lo : lo + HEAD, :]]
                if h4:
                    parts.insert(0, jnp.zeros((h4 * HEAD, tokens), BF16))
                if h4 < 128 // HEAD - 1:
                    parts.append(jnp.zeros((128 - (h4 + 1) * HEAD, tokens), BF16))
                s = jnp.dot(kb, jnp.concatenate(parts, axis=0), preferred_element_type=F32)
                s_car = s[tokens : tokens + 1]
                s = s[:tokens]
                top = jnp.maximum(jnp.max(s, axis=0, keepdims=True), s_car)
                e = jnp.exp2((s - top) * sharp)
                e_car = jnp.exp2((s_car - top) * sharp)
                total = jnp.sum(e, axis=0, keepdims=True) + e_car
                o = jnp.dot(v_t[lo : lo + HEAD, :], e.astype(BF16), preferred_element_type=F32)
                o = o + vcar_col[lo : lo + HEAD] * e_car.astype(BF16).astype(F32)
                in_t[lo : lo + HEAD, :] = (o / total + glob_col[lo : lo + HEAD]).astype(BF16)
        inner = in_t[...].T
        upd = jnp.dot(inner, wo_ref[...], preferred_element_type=F32).astype(BF16)
        ybuf[slot] = upd.reshape(npos, rows, WIN * WIN, width)
        for p in reversed(window_peers(my_pos, npos) + [my_pos]):
            dst = ci * npos + p

            @pl.when(dst != me)
            def _():
                b_copy(slot, p, dst, me, j).start()

            @pl.when(dst == me)
            def _():
                bl_copy(slot, j).start()

        return carry

    lax.fori_loop(0, own, cube, 0)

    for k, d in enumerate(peers):
        p_copy(k, d, me).wait_send()
        g_copy(k, d, me).wait_send()
    for k, d in enumerate(in_peers):
        c_copy(k, d, ii).wait_send()
    for j in range(span):
        for k, d in enumerate(peers):
            f_copy(k, j, d, me).wait_send()
    for j in range(span):
        for d in peers:
            b_copy(0, 0, me, d, j).wait_recv()
        bl_copy(my_ci * span + j, j).wait()
    for slot in range(own):
        for p in range(npos):
            dst = (slot // span) * npos + p

            @pl.when(dst != me)
            def _():
                b_copy(slot, p, dst, me, slot % span).wait_send()


def body(n_in, n_win, tokens, w, w_out):
    rows, xl, dep, width = tokens.shape
    strips = xl // WIN
    npos = WIN // rows
    span = strips // n_win
    own = span * (n_win // npos)
    group_cars = (n_win // npos) * strips
    cube = WIN * WIN * WIN
    block = (rows, WIN * WIN, width)
    hbm = pl.BlockSpec(memory_space=pl.ANY)
    dma = pltpu.SemaphoreType.DMA
    shaped = tokens.reshape(rows, strips, WIN * dep, width)
    out = pl.pallas_call(
        functools.partial(kernel, n_in, n_win, rows, strips),
        out_shape=jax.ShapeDtypeStruct(shaped.shape, BF16),
        in_specs=[hbm, hbm, hbm],
        out_specs=pl.BlockSpec(memory_space=pl.ANY),
        scratch_shapes=[
            pltpu.VMEM((strips,) + block, BF16),
            pltpu.VMEM(w.shape, BF16),
            pltpu.VMEM(w_out.shape, BF16),
            pltpu.VMEM((strips,) + block, BF16),
            pltpu.VMEM((own, npos) + block, BF16),
            pltpu.VMEM((own, npos) + block, BF16),
            pltpu.VMEM((n_win, n_win, span, width), F32),
            pltpu.VMEM((n_win, n_win // npos, span, width), F32),
            pltpu.VMEM((group_cars, width), F32),
            pltpu.VMEM((n_in, group_cars, width), BF16),
            pltpu.VMEM((width, width), BF16),
            pltpu.VMEM((width, width), BF16),
            pltpu.VMEM((cube + 16, width), BF16),
            pltpu.VMEM((width, cube), BF16),
            pltpu.VMEM((width, cube), BF16),
            pltpu.VMEM((width, cube), BF16),
            pltpu.VMEM((group_cars, width), F32),
            pltpu.VMEM((group_cars, width), F32),
            pltpu.VMEM((group_cars, width), F32),
            dma((n_win, span)),
            dma((n_win, span)),
            dma((own, npos)),
            dma((n_win, span)),
            dma((n_win,)),
            dma((n_win,)),
            dma((n_win,)),
            dma((n_win,)),
            dma((n_in,)),
            dma((n_in,)),
            dma((span,)),
            dma((span,)),
            dma((strips,)),
            dma((2,)),
        ],
        compiler_params=pltpu.CompilerParams(
            collective_id=0, has_side_effects=True, vmem_limit_bytes=36 * 1024 * 1024
        ),
        cost_estimate=pl.CostEstimate(
            flops=2 * own * cube * width * (4 * width + 2 * cube),
            bytes_accessed=4 * own * cube * width,
            transcendentals=own * FOCUS_GROUPS * cube * cube,
        ),
    )(*(pltpu.with_memory_space_constraint(a, pltpu.HBM) for a in (shaped, w, w_out)))
    return out.reshape(tokens.shape)


def solution(mesh):
    return jax.shard_map(
        functools.partial(body, mesh.shape["inline"], mesh.shape["window"]),
        mesh=mesh,
        in_specs=(P(("replica", "inline", "window"), None, None, None), P(), P()),
        out_specs=P(("replica", "inline", "window"), None, None, None),
        check_vma=False,
    )
```

```python
import functools

import jax
import jax.numpy as jnp
from jax import lax
from jax.experimental import pallas as pl
from jax.experimental.pallas import tpu as pltpu
from jax.sharding import PartitionSpec as P

EMBED_SPAN = 512
FOCUS_GROUPS = 16
HEAD = EMBED_SPAN // FOCUS_GROUPS
WIN = 8
EPSILON = 1e-05
LOG2_E = 1.4426950408889634
MESH = pl.DeviceIdType.MESH
F32 = jnp.float32
BF16 = jnp.bfloat16


def standardize(x):
    center = x - jnp.mean(x, axis=-1, keepdims=True)
    spread = jnp.mean(center * center, axis=-1, keepdims=True)
    return center * lax.rsqrt(spread + EPSILON)


def window_peers(me, n):
    if n % 2:
        return [lax.rem(me + o, n) for o in range(1, n)]
    same = [lax.rem(me + o, n) for o in range(2, n, 2)]
    odd = [lax.rem(n + c - me, n) for c in range(n - 1, 0, -2)]
    return same + odd


def kernel(
    n_in, n_win, rows, strips,
    tok_ref, w_hbm, wo_hbm, out_ref,
    tok_buf, w_ref, wo_ref,
    normed, xin, ybuf, psum, cars, wq_t, wv_t, k_buf, q_t, v_t, in_t, glob_buf, qcar_buf, kcar_buf, vcar_buf,
    fsend, frecv, bsend, brecv, psend, precv, csend, crecv, lsem, blsem, tsem, wsem,
):
    ii = lax.axis_index("inline")
    me = lax.axis_index("window")
    span = strips // n_win
    npos = WIN // rows
    n_ci = n_win // npos
    own = span * n_ci
    group_cars = n_ci * strips
    width = EMBED_SPAN
    tokens = WIN * WIN * WIN
    my_ci = me // npos
    my_pos = lax.rem(me, npos)
    peers = window_peers(me, n_win)
    in_peers = [lax.rem(ii + o, n_in) for o in range(1, n_in)]

    barrier = pltpu.get_barrier_semaphore()
    for d in peers:
        pl.semaphore_signal(barrier, inc=1, device_id={"window": d}, device_id_type=MESH)
    for d in in_peers:
        pl.semaphore_signal(barrier, inc=1, device_id={"inline": d}, device_id_type=MESH)

    order = [(j, k, d) for j in range(span) for k, d in enumerate(peers + [me])]

    def t_copy(n):
        j, _, d = order[n]
        return pltpu.make_async_copy(tok_ref.at[:, d * span + j], tok_buf.at[n], tsem.at[n])

    for n in range(len(order)):
        t_copy(n).start()
    w_copy = pltpu.make_async_copy(w_hbm, w_ref, wsem.at[0])
    wo_copy = pltpu.make_async_copy(wo_hbm, wo_ref, wsem.at[1])
    w_copy.start()
    wo_copy.start()

    def p_copy(k, d, src):
        return pltpu.make_async_remote_copy(
            src_ref=psum.at[src], dst_ref=psum.at[src], send_sem=psend.at[k], recv_sem=precv.at[src],
            device_id={"window": d}, device_id_type=MESH,
        )

    def f_copy(k, j, d, src):
        return pltpu.make_async_remote_copy(
            src_ref=normed.at[d * span + j], dst_ref=xin.at[(src // npos) * span + j, lax.rem(src, npos)],
            send_sem=fsend.at[k, j], recv_sem=frecv.at[src, j],
            device_id={"window": d}, device_id_type=MESH,
        )

    def l_copy(j):
        return pltpu.make_async_copy(
            normed.at[me * span + j], xin.at[my_ci * span + j, my_pos], lsem.at[j]
        )

    for n, (j, k, d) in enumerate(order):
        t_copy(n).wait()
        x = standardize(tok_buf[n].astype(F32)).astype(BF16)
        normed[d * span + j] = x
        psum[me, pl.ds(d * span + j, 1), :] = jnp.sum(x.astype(F32), axis=(0, 1))[None, :]
        if n == 0:
            pl.semaphore_wait(barrier, len(peers) + len(in_peers))
        if j == 0:
            if k == len(peers):
                l_copy(j).start()
            else:
                f_copy(k, j, d, me).start()
    for k, d in enumerate(peers):
        p_copy(k, d, me).start()
    for j, k, d in order:
        if j:
            if k == len(peers):
                l_copy(j).start()
            else:
                f_copy(k, j, d, me).start()
    w_copy.wait()
    wo_copy.wait()

    wq_t[...] = w_ref[:, :width].T
    wv_t[...] = w_ref[:, 2 * width :].T

    for d in peers:
        p_copy(0, d, d).wait_recv()
    for ci in range(n_ci):
        total = psum[ci * npos]
        for p in range(1, npos):
            total = total + psum[ci * npos + p]
        cars[ii, pl.ds(ci * strips, strips), :] = standardize(total * (1.0 / tokens)).astype(BF16)

    def c_copy(k, d, src):
        return pltpu.make_async_remote_copy(
            src_ref=cars.at[src], dst_ref=cars.at[src], send_sem=csend.at[k], recv_sem=crecv.at[src],
            device_id={"inline": d}, device_id_type=MESH,
        )

    for k, d in enumerate(in_peers):
        c_copy(k, d, ii).start()

    scale = HEAD ** (-0.5)
    sharp = scale * LOG2_E
    mine = jnp.dot(cars[ii], w_ref[...], preferred_element_type=F32).astype(BF16)
    kcar_buf[...] = mine[:, width : 2 * width].astype(F32)
    vcar_buf[...] = mine[:, 2 * width :].astype(F32)
    qcar_buf[...] = mine[:, :width].astype(F32)

    def global_part():
        for d in in_peers:
            c_copy(0, d, d).wait_recv()
        every = cars[...].reshape(n_in * group_cars, width)
        kv = jnp.dot(every, w_ref[:, width:], preferred_element_type=F32).astype(BF16)
        col_head = lax.broadcasted_iota(jnp.int32, (group_cars, width), 1) // HEAD
        q_car = qcar_buf[...]
        glob = jnp.zeros((group_cars, width), F32)
        for h in range(FOCUS_GROUPS):
            q_h = jnp.where(col_head == h, q_car, 0.0).astype(BF16)
            s = lax.dot_general(q_h, kv[:, :width], (((1,), (1,)), ((), ())), preferred_element_type=F32) * scale
            e = jnp.exp(s - jnp.max(s, axis=-1, keepdims=True))
            t = jnp.sum(e, axis=-1, keepdims=True)
            o = jnp.dot(e.astype(BF16), kv[:, width:], preferred_element_type=F32) / t
            glob = jnp.where(col_head == h, o, glob)
        glob_buf[...] = glob

    def b_copy(slot, p, dst, owner, j):
        return pltpu.make_async_remote_copy(
            src_ref=ybuf.at[slot, p], dst_ref=out_ref.at[:, owner * span + j],
            send_sem=bsend.at[slot, p], recv_sem=brecv.at[owner, j],
            device_id={"window": dst}, device_id_type=MESH,
        )

    def bl_copy(slot, j):
        return pltpu.make_async_copy(ybuf.at[slot, my_pos], out_ref.at[:, me * span + j], blsem.at[j])

    def cube(slot, carry):
        ci = slot // span
        j = lax.rem(slot, span)
        for p in range(npos):
            src = ci * npos + p

            @pl.when(src != me)
            def _():
                f_copy(0, j, me, src).wait_recv()

            @pl.when(src == me)
            def _():
                l_copy(j).wait()

        x = xin[slot].reshape(tokens, width)
        row = ci * strips + me * span + j
        pick = lax.broadcasted_iota(jnp.int32, (group_cars, width), 0) == row

        def chosen(ref):
            return jnp.sum(jnp.where(pick, ref[...], 0.0), axis=0, keepdims=True)

        def column(r):
            return jnp.broadcast_to(r, (128, width)).T[:, :1]

        k_buf[:tokens, :] = jnp.dot(x, w_ref[:, width : 2 * width], preferred_element_type=F32).astype(BF16)
        k_buf[tokens:, :] = jnp.broadcast_to(chosen(kcar_buf), (16, width)).astype(BF16)
        nt = (((1,), (1,)), ((), ()))
        q_t[...] = lax.dot_general(wq_t[...], x, nt, preferred_element_type=F32).astype(BF16)
        v_t[...] = lax.dot_general(wv_t[...], x, nt, preferred_element_type=F32).astype(BF16)
        vcar_col = column(chosen(vcar_buf))
        for hb in range(width // 128):
            kb = k_buf[:, hb * 128 : (hb + 1) * 128]
            for h4 in range(128 // HEAD):
                lo = hb * 128 + h4 * HEAD
                parts = [q_t[lo : lo + HEAD, :]]
                if h4:
                    parts.insert(0, jnp.zeros((h4 * HEAD, tokens), BF16))
                if h4 < 128 // HEAD - 1:
                    parts.append(jnp.zeros((128 - (h4 + 1) * HEAD, tokens), BF16))
                s = jnp.dot(kb, jnp.concatenate(parts, axis=0), preferred_element_type=F32)
                s_car = s[tokens : tokens + 1]
                s = s[:tokens]
                top = jnp.maximum(jnp.max(s, axis=0, keepdims=True), s_car)
                e = jnp.exp2((s - top) * sharp)
                e_car = jnp.exp2((s_car - top) * sharp)
                v_one = jnp.concatenate([v_t[lo : lo + HEAD, :], jnp.ones((16, tokens), BF16)], axis=0)
                o = jnp.dot(v_one, e.astype(BF16), preferred_element_type=F32)
                total = o[HEAD : HEAD + 1] + e_car
                o = o[:HEAD] + vcar_col[lo : lo + HEAD] * e_car.astype(BF16).astype(F32)
                in_t[lo : lo + HEAD, :] = o / total

        pl.when(slot == 0)(global_part)
        inner = (in_t[...] + column(chosen(glob_buf))).astype(BF16).T
        upd = jnp.dot(inner, wo_ref[...], preferred_element_type=F32).astype(BF16)
        ybuf[slot] = upd.reshape(npos, rows, WIN * WIN, width)
        for p in window_peers(my_pos, npos) + [my_pos]:
            dst = ci * npos + p

            @pl.when(dst != me)
            def _():
                b_copy(slot, p, dst, me, j).start()

            @pl.when(dst == me)
            def _():
                bl_copy(slot, j).start()

        return carry

    lax.fori_loop(0, own, cube, 0)

    for k, d in enumerate(peers):
        p_copy(k, d, me).wait_send()
    for k, d in enumerate(in_peers):
        c_copy(k, d, ii).wait_send()
    for j in range(span):
        for k, d in enumerate(peers):
            f_copy(k, j, d, me).wait_send()
    for j in range(span):
        for d in peers:
            b_copy(0, 0, me, d, j).wait_recv()
        bl_copy(my_ci * span + j, j).wait()
    for slot in range(own):
        for p in range(npos):
            dst = (slot // span) * npos + p

            @pl.when(dst != me)
            def _():
                b_copy(slot, p, dst, me, slot % span).wait_send()


def body(n_in, n_win, tokens, w, w_out):
    rows, xl, dep, width = tokens.shape
    strips = xl // WIN
    npos = WIN // rows
    span = strips // n_win
    own = span * (n_win // npos)
    group_cars = (n_win // npos) * strips
    cube = WIN * WIN * WIN
    block = (rows, WIN * WIN, width)
    hbm = pl.BlockSpec(memory_space=pl.ANY)
    dma = pltpu.SemaphoreType.DMA
    shaped = tokens.reshape(rows, strips, WIN * dep, width)
    out = pl.pallas_call(
        functools.partial(kernel, n_in, n_win, rows, strips),
        out_shape=jax.ShapeDtypeStruct(shaped.shape, BF16),
        in_specs=[hbm, hbm, hbm],
        out_specs=pl.BlockSpec(memory_space=pl.ANY),
        scratch_shapes=[
            pltpu.VMEM((strips,) + block, BF16),
            pltpu.VMEM(w.shape, BF16),
            pltpu.VMEM(w_out.shape, BF16),
            pltpu.VMEM((strips,) + block, BF16),
            pltpu.VMEM((own, npos) + block, BF16),
            pltpu.VMEM((own, npos) + block, BF16),
            pltpu.VMEM((n_win, strips, width), F32),
            pltpu.VMEM((n_in, group_cars, width), BF16),
            pltpu.VMEM((width, width), BF16),
            pltpu.VMEM((width, width), BF16),
            pltpu.VMEM((cube + 16, width), BF16),
            pltpu.VMEM((width, cube), BF16),
            pltpu.VMEM((width, cube), BF16),
            pltpu.VMEM((width, cube), F32),
            pltpu.VMEM((group_cars, width), F32),
            pltpu.VMEM((group_cars, width), F32),
            pltpu.VMEM((group_cars, width), F32),
            pltpu.VMEM((group_cars, width), F32),
            dma((n_win, span)),
            dma((n_win, span)),
            dma((own, npos)),
            dma((n_win, span)),
            dma((n_win,)),
            dma((n_win,)),
            dma((n_in,)),
            dma((n_in,)),
            dma((span,)),
            dma((span,)),
            dma((strips,)),
            dma((2,)),
        ],
        compiler_params=pltpu.CompilerParams(
            collective_id=0, has_side_effects=True, vmem_limit_bytes=36 * 1024 * 1024
        ),
        cost_estimate=pl.CostEstimate(
            flops=2 * own * cube * width * (4 * width + 2 * cube),
            bytes_accessed=4 * own * cube * width,
            transcendentals=own * FOCUS_GROUPS * cube * cube,
        ),
    )(*(pltpu.with_memory_space_constraint(a, pltpu.HBM) for a in (shaped, w, w_out)))
    return out.reshape(tokens.shape)


def solution(mesh):
    return jax.shard_map(
        functools.partial(body, mesh.shape["inline"], mesh.shape["window"]),
        mesh=mesh,
        in_specs=(P(("replica", "inline", "window"), None, None, None), P(), P()),
        out_specs=P(("replica", "inline", "window"), None, None, None),
        check_vma=False,
    )
```

```python
import functools

import jax
import jax.numpy as jnp
from jax import lax
from jax.experimental import pallas as pl
from jax.experimental.pallas import tpu as pltpu
from jax.sharding import PartitionSpec as P

EMBED_SPAN = 512
FOCUS_GROUPS = 16
HEAD = EMBED_SPAN // FOCUS_GROUPS
WIN = 8
EPSILON = 1e-05
LOG2_E = 1.4426950408889634
MESH = pl.DeviceIdType.MESH
F32 = jnp.float32
BF16 = jnp.bfloat16


def standardize(x):
    center = x - jnp.mean(x, axis=-1, keepdims=True)
    spread = jnp.mean(center * center, axis=-1, keepdims=True)
    return center * lax.rsqrt(spread + EPSILON)


def window_peers(me, n):
    if n % 2:
        return [lax.rem(me + o, n) for o in range(1, n)]
    same = [lax.rem(me + o, n) for o in range(2, n, 2)]
    odd = [lax.rem(n + c - me, n) for c in range(n - 1, 0, -2)]
    return same + odd


def kernel(
    n_in, n_win, rows, strips,
    tok_ref, w_hbm, wo_hbm, out_ref,
    tok_buf, w_ref, wo_ref,
    normed, xin, ybuf, psum, own_cars, all_cars, cars, wq_t, wv_t, k_buf, q_t, v_t, in_t, glob_buf, qcar_buf, kcar_buf, vcar_buf,
    fsend, frecv, bsend, brecv, psend, precv, gsend, grecv, csend, crecv, lsem, blsem, tsem, wsem,
):
    ii = lax.axis_index("inline")
    me = lax.axis_index("window")
    span = strips // n_win
    npos = WIN // rows
    n_ci = n_win // npos
    own = span * n_ci
    group_cars = n_ci * strips
    width = EMBED_SPAN
    tokens = WIN * WIN * WIN
    my_ci = me // npos
    my_pos = lax.rem(me, npos)
    peers = window_peers(me, n_win)
    in_peers = [lax.rem(ii + o, n_in) for o in range(1, n_in)]

    barrier = pltpu.get_barrier_semaphore()
    for d in peers:
        pl.semaphore_signal(barrier, inc=1, device_id={"window": d}, device_id_type=MESH)
    for d in in_peers:
        pl.semaphore_signal(barrier, inc=1, device_id={"inline": d}, device_id_type=MESH)

    order = [(j, k, d) for j in range(span) for k, d in enumerate(peers + [me])]

    def t_copy(n):
        j, _, d = order[n]
        return pltpu.make_async_copy(tok_ref.at[:, d * span + j], tok_buf.at[n], tsem.at[n])

    for n in range(len(order)):
        t_copy(n).start()
    w_copy = pltpu.make_async_copy(w_hbm, w_ref, wsem.at[0])
    wo_copy = pltpu.make_async_copy(wo_hbm, wo_ref, wsem.at[1])
    w_copy.start()
    wo_copy.start()

    def p_copy(k, d, src):
        return pltpu.make_async_remote_copy(
            src_ref=psum.at[src, d], dst_ref=psum.at[src, d], send_sem=psend.at[k], recv_sem=precv.at[src],
            device_id={"window": d}, device_id_type=MESH,
        )

    def f_copy(k, j, d, src):
        return pltpu.make_async_remote_copy(
            src_ref=normed.at[d * span + j], dst_ref=xin.at[(src // npos) * span + j, lax.rem(src, npos)],
            send_sem=fsend.at[k, j], recv_sem=frecv.at[src, j],
            device_id={"window": d}, device_id_type=MESH,
        )

    def l_copy(j):
        return pltpu.make_async_copy(
            normed.at[me * span + j], xin.at[my_ci * span + j, my_pos], lsem.at[j]
        )

    for n, (j, k, d) in enumerate(order):
        t_copy(n).wait()
        x = standardize(tok_buf[n].astype(F32)).astype(BF16)
        normed[d * span + j] = x
        psum[me, d, pl.ds(j, 1), :] = jnp.sum(x.astype(F32), axis=(0, 1))[None, :]
        if n == 0:
            pl.semaphore_wait(barrier, len(peers) + len(in_peers))
        if j == 0:
            if k == len(peers):
                l_copy(j).start()
            else:
                f_copy(k, j, d, me).start()
    for k, d in enumerate(peers):
        p_copy(k, d, me).start()

    def send_round(j):
        for k, d in enumerate(peers):
            f_copy(k, j, d, me).start()
        l_copy(j).start()

    if span > 1:
        send_round(1)
    w_copy.wait()
    wo_copy.wait()

    wq_t[...] = w_ref[:, :width].T
    wv_t[...] = w_ref[:, 2 * width :].T

    def g_copy(k, d, src):
        return pltpu.make_async_remote_copy(
            src_ref=own_cars.at[src], dst_ref=own_cars.at[src], send_sem=gsend.at[k], recv_sem=grecv.at[src],
            device_id={"window": d}, device_id_type=MESH,
        )

    for d in peers:
        p_copy(0, me, d).wait_recv()
    for ci in range(n_ci):
        total = psum[ci * npos, me]
        for p in range(1, npos):
            total = total + psum[ci * npos + p, me]
        own_cars[me, ci] = standardize(total * (1.0 / tokens))
    for k, d in enumerate(peers):
        g_copy(k, d, me).start()
    for j in range(2, span):
        send_round(j)
    for d in peers:
        g_copy(0, me, d).wait_recv()
    for ci in range(n_ci):
        for w in range(n_win):
            first = ci * strips + w * span
            all_cars[first : first + span, :] = own_cars[w, ci]
    cars[ii] = all_cars[...].astype(BF16)

    def c_copy(k, d, src):
        return pltpu.make_async_remote_copy(
            src_ref=cars.at[src], dst_ref=cars.at[src], send_sem=csend.at[k], recv_sem=crecv.at[src],
            device_id={"inline": d}, device_id_type=MESH,
        )

    for k, d in enumerate(in_peers):
        c_copy(k, d, ii).start()

    scale = HEAD ** (-0.5)
    sharp = scale * LOG2_E
    mine = jnp.dot(cars[ii], w_ref[...], preferred_element_type=F32).astype(BF16)
    kcar_buf[...] = mine[:, width : 2 * width].astype(F32)
    vcar_buf[...] = mine[:, 2 * width :].astype(F32)
    qcar_buf[...] = mine[:, :width].astype(F32)

    def global_part():
        for d in in_peers:
            c_copy(0, d, d).wait_recv()
        every = cars[...].reshape(n_in * group_cars, width)
        kv = jnp.dot(every, w_ref[:, width:], preferred_element_type=F32).astype(BF16)
        col_head = lax.broadcasted_iota(jnp.int32, (group_cars, width), 1) // HEAD
        q_car = qcar_buf[...]
        glob = jnp.zeros((group_cars, width), F32)
        for h in range(FOCUS_GROUPS):
            q_h = jnp.where(col_head == h, q_car, 0.0).astype(BF16)
            s = lax.dot_general(q_h, kv[:, :width], (((1,), (1,)), ((), ())), preferred_element_type=F32) * scale
            e = jnp.exp(s - jnp.max(s, axis=-1, keepdims=True))
            t = jnp.sum(e, axis=-1, keepdims=True)
            o = jnp.dot(e.astype(BF16), kv[:, width:], preferred_element_type=F32) / t
            glob = jnp.where(col_head == h, o, glob)
        glob_buf[...] = glob

    def b_copy(slot, p, dst, owner, j):
        return pltpu.make_async_remote_copy(
            src_ref=ybuf.at[slot, p], dst_ref=out_ref.at[:, owner * span + j],
            send_sem=bsend.at[slot, p], recv_sem=brecv.at[owner, j],
            device_id={"window": dst}, device_id_type=MESH,
        )

    def bl_copy(slot, j):
        return pltpu.make_async_copy(ybuf.at[slot, my_pos], out_ref.at[:, me * span + j], blsem.at[j])

    def cube(slot, carry):
        ci = slot // span
        j = lax.rem(slot, span)
        for p in range(npos):
            src = ci * npos + p

            @pl.when(src != me)
            def _():
                f_copy(0, j, me, src).wait_recv()

            @pl.when(src == me)
            def _():
                l_copy(j).wait()

        x = xin[slot].reshape(tokens, width)
        row = ci * strips + me * span + j
        pick = lax.broadcasted_iota(jnp.int32, (group_cars, width), 0) == row

        def chosen(ref):
            return jnp.sum(jnp.where(pick, ref[...], 0.0), axis=0, keepdims=True)

        def column(r):
            return jnp.broadcast_to(r, (128, width)).T[:, :1]

        k_buf[:tokens, :] = jnp.dot(x, w_ref[:, width : 2 * width], preferred_element_type=F32).astype(BF16)
        k_buf[tokens:, :] = jnp.broadcast_to(chosen(kcar_buf), (16, width)).astype(BF16)
        nt = (((1,), (1,)), ((), ()))
        q_t[...] = lax.dot_general(wq_t[...], x, nt, preferred_element_type=F32).astype(BF16)
        v_t[...] = lax.dot_general(wv_t[...], x, nt, preferred_element_type=F32).astype(BF16)
        vcar_col = column(chosen(vcar_buf))
        for hb in range(width // 128):
            kb = k_buf[:, hb * 128 : (hb + 1) * 128]
            for h4 in range(128 // HEAD):
                lo = hb * 128 + h4 * HEAD
                parts = [q_t[lo : lo + HEAD, :]]
                if h4:
                    parts.insert(0, jnp.zeros((h4 * HEAD, tokens), BF16))
                if h4 < 128 // HEAD - 1:
                    parts.append(jnp.zeros((128 - (h4 + 1) * HEAD, tokens), BF16))
                s = jnp.dot(kb, jnp.concatenate(parts, axis=0), preferred_element_type=F32)
                s_car = s[tokens : tokens + 1]
                s = s[:tokens]
                top = jnp.maximum(jnp.max(s, axis=0, keepdims=True), s_car)
                e = jnp.exp2((s - top) * sharp)
                e_car = jnp.exp2((s_car - top) * sharp)
                v_one = jnp.concatenate([v_t[lo : lo + HEAD, :], jnp.ones((16, tokens), BF16)], axis=0)
                o = jnp.dot(v_one, e.astype(BF16), preferred_element_type=F32)
                total = o[HEAD : HEAD + 1] + e_car
                o = o[:HEAD] + vcar_col[lo : lo + HEAD] * e_car.astype(BF16).astype(F32)
                in_t[lo : lo + HEAD, :] = o / total

        pl.when(slot == 0)(global_part)
        inner = (in_t[...] + column(chosen(glob_buf))).astype(BF16).T
        upd = jnp.dot(inner, wo_ref[...], preferred_element_type=F32).astype(BF16)
        ybuf[slot] = upd.reshape(npos, rows, WIN * WIN, width)
        for p in window_peers(my_pos, npos) + [my_pos]:
            dst = ci * npos + p

            @pl.when(dst != me)
            def _():
                b_copy(slot, p, dst, me, j).start()

            @pl.when(dst == me)
            def _():
                bl_copy(slot, j).start()

        return carry

    lax.fori_loop(0, own, cube, 0)

    for k, d in enumerate(peers):
        p_copy(k, d, me).wait_send()
        g_copy(k, d, me).wait_send()
    for k, d in enumerate(in_peers):
        c_copy(k, d, ii).wait_send()
    for j in range(span):
        for k, d in enumerate(peers):
            f_copy(k, j, d, me).wait_send()
    for j in range(span):
        for d in peers:
            b_copy(0, 0, me, d, j).wait_recv()
        bl_copy(my_ci * span + j, j).wait()
    for slot in range(own):
        for p in range(npos):
            dst = (slot // span) * npos + p

            @pl.when(dst != me)
            def _():
                b_copy(slot, p, dst, me, slot % span).wait_send()


def body(n_in, n_win, tokens, w, w_out):
    rows, xl, dep, width = tokens.shape
    strips = xl // WIN
    npos = WIN // rows
    span = strips // n_win
    own = span * (n_win // npos)
    group_cars = (n_win // npos) * strips
    cube = WIN * WIN * WIN
    block = (rows, WIN * WIN, width)
    hbm = pl.BlockSpec(memory_space=pl.ANY)
    dma = pltpu.SemaphoreType.DMA
    shaped = tokens.reshape(rows, strips, WIN * dep, width)
    out = pl.pallas_call(
        functools.partial(kernel, n_in, n_win, rows, strips),
        out_shape=jax.ShapeDtypeStruct(shaped.shape, BF16),
        in_specs=[hbm, hbm, hbm],
        out_specs=pl.BlockSpec(memory_space=pl.ANY),
        scratch_shapes=[
            pltpu.VMEM((strips,) + block, BF16),
            pltpu.VMEM(w.shape, BF16),
            pltpu.VMEM(w_out.shape, BF16),
            pltpu.VMEM((strips,) + block, BF16),
            pltpu.VMEM((own, npos) + block, BF16),
            pltpu.VMEM((own, npos) + block, BF16),
            pltpu.VMEM((n_win, n_win, span, width), F32),
            pltpu.VMEM((n_win, n_win // npos, span, width), F32),
            pltpu.VMEM((group_cars, width), F32),
            pltpu.VMEM((n_in, group_cars, width), BF16),
            pltpu.VMEM((width, width), BF16),
            pltpu.VMEM((width, width), BF16),
            pltpu.VMEM((cube + 16, width), BF16),
            pltpu.VMEM((width, cube), BF16),
            pltpu.VMEM((width, cube), BF16),
            pltpu.VMEM((width, cube), F32),
            pltpu.VMEM((group_cars, width), F32),
            pltpu.VMEM((group_cars, width), F32),
            pltpu.VMEM((group_cars, width), F32),
            pltpu.VMEM((group_cars, width), F32),
            dma((n_win, span)),
            dma((n_win, span)),
            dma((own, npos)),
            dma((n_win, span)),
            dma((n_win,)),
            dma((n_win,)),
            dma((n_win,)),
            dma((n_win,)),
            dma((n_in,)),
            dma((n_in,)),
            dma((span,)),
            dma((span,)),
            dma((strips,)),
            dma((2,)),
        ],
        compiler_params=pltpu.CompilerParams(
            collective_id=0, has_side_effects=True, vmem_limit_bytes=36 * 1024 * 1024
        ),
        cost_estimate=pl.CostEstimate(
            flops=2 * own * cube * width * (4 * width + 2 * cube),
            bytes_accessed=4 * own * cube * width,
            transcendentals=own * FOCUS_GROUPS * cube * cube,
        ),
    )(*(pltpu.with_memory_space_constraint(a, pltpu.HBM) for a in (shaped, w, w_out)))
    return out.reshape(tokens.shape)


def solution(mesh):
    return jax.shard_map(
        functools.partial(body, mesh.shape["inline"], mesh.shape["window"]),
        mesh=mesh,
        in_specs=(P(("replica", "inline", "window"), None, None, None), P(), P()),
        out_specs=P(("replica", "inline", "window"), None, None, None),
        check_vma=False,
    )
```
